256 devices in a mesh: inner: 16 (over z_hi, y), outer: 16 (over x, z_lo, core).
Axes of the slice: x: 4, y: 4, z: 8 (z_hi: 4, z_lo: 2; z = z_hi * 2 + z_lo), core: 2. Of those that a mesh axis runs over, the one named last changes fastest.
Arguments:
- frames: bfloat16 [16, 96, 64, 2048], P('outer', 'inner'), may hold values from -6 to 6
- queries: bfloat16 [16, 96, 64, 1024], P('outer', 'inner'), may hold values from -160 to 160
- w_keyval: bfloat16 [2048, 2048], replicated, may hold values from -0.125 to 0.125
- bucket_table: int32 [54], replicated, may hold values from 0 to 31
- bias_table: float32 [32, 8], replicated, may hold values from -4 to 4
- block_mask: int32 [16, 16, 9], P('outer', 'inner'), may hold values 0 or 1
Outputs:
- attended: bfloat16 [16, 96, 64, 1024], P('outer', 'inner')
The draws below stay inside these ranges and needn't reach their ends.
All inputs are finite; a program needn't handle non-finite values. No bound on the sum of `block_mask` on one device may be relied on, other than what follows from the above.
Results may differ from the reference program's by a relative error of at most 0.011.
Values may be sent and summed in bfloat16 or wider, within the bound.
No kernel may reach another device: no remote copies, remote signals or barrier semaphores. Data moves between devices by JAX's collectives and lax.ppermute only.
A program may use at most 192 MiB of HBM per device.

```python
import jax
import jax.numpy as jnp
from jax import lax

D = 2048
HEADS = 8
HEAD = 128
SPATIAL = 64
BUCKETS = 32
SPAN = 8
FR_DEV = 6
CYCLE_FRAMES = 96
MAXOFF = 54
N_INNER = 16
N_OUTER = 16


def draw_queries(key, part):
    key = jax.random.fold_in(key, 11)
    shape = (N_OUTER, N_INNER * FR_DEV, SPATIAL, HEADS * HEAD)
    values = jnp.clip(jax.random.normal(jax.random.fold_in(key, 1), shape, jnp.float32), -4.0, 4.0)
    return values.astype(jnp.bfloat16)


def with_ends(values, key, low, largest):
    longest = values.shape.index(max(values.shape))
    spots = []
    for shift in (0, 1):
        where = [jax.random.randint(jax.random.fold_in(key, axis), (), 0, length) for axis, length in enumerate(values.shape)]
        where[longest] = (where[longest] + shift) % values.shape[longest]
        spots.append(tuple(where))
    return values.at[spots[0]].set(low).at[spots[1]].set(largest)


def level_of(key, shape, cuts, smallest, largest):
    gain, own = 1.0, jax.random.fold_in(key, 6)
    for dim, parts in cuts:
        draws = jnp.exp(jax.random.uniform(jax.random.fold_in(own, dim), (parts,), jnp.float32, smallest / len(cuts), largest / len(cuts)))
        gain = gain * jnp.repeat(draws, shape[dim] // parts).reshape([-1 if axis == dim else 1 for axis in range(len(shape))])
    return gain


def scatter_about(own_key, shape, scale, reach, cuts=(), held_as=jnp.bfloat16):
    entries = jax.random.normal(own_key, shape, jnp.float32) * scale
    if len(cuts) > 0:
        entries = level_of(own_key, shape, cuts, -0.22, 0.18) * entries
    return jnp.clip(entries, min=-reach, max=reach).astype(held_as)


def setup_inputs(seed: int = 0) -> dict:
    key_of = jax.random.split(jax.random.key(seed), 7)
    return {
        "frames": scatter_about(key_of[0], (N_OUTER, CYCLE_FRAMES, SPATIAL, D), 1.0, 6.0, ((0, 16), (1, 16))),
        "queries": draw_queries(jax.random.fold_in(key_of[6], 71), 0),
        "w_keyval": scatter_about(key_of[2], (D, 2 * HEADS * HEAD), D ** -0.5, 0.125),
        "bucket_table": with_ends(jax.random.randint(key_of[3], (MAXOFF,), 0, BUCKETS), jax.random.fold_in(key_of[3], 1), 0, BUCKETS - 1).astype(jnp.int32),
        "bias_table": scatter_about(key_of[4], (BUCKETS, HEADS), 1.0, 4.0, (), jnp.float32),
        "block_mask": with_ends((jax.random.randint(key_of[5], (N_OUTER, N_INNER, SPAN + 1), 0, 4) < 3).astype(jnp.int32), jax.random.fold_in(key_of[5], 1), 0, 1),
    }


def bias_terms(bucket_table, bias_table, frame_count, reach_count):
    table = jnp.dot(jax.nn.one_hot(bucket_table, bias_table.shape[0], dtype=jnp.float32), bias_table, precision=lax.Precision.HIGHEST)
    query_pos = jnp.arange(frame_count, dtype=jnp.int32)[:, None, None]
    reach_pos = jnp.arange(reach_count, dtype=jnp.int32)[None, :, None]
    key_pos = jnp.arange(frame_count, dtype=jnp.int32)[None, None, :]
    offsets = query_pos - key_pos + reach_pos * frame_count
    picked = jax.nn.one_hot(offsets, table.shape[0], dtype=jnp.float32)
    bias = jnp.einsum('fmgo,oh->hfmg', picked, table, precision=lax.Precision.HIGHEST)
    return bias, query_pos, reach_pos, key_pos


def attend(query, window, bucket_table, bias_table, mask_row, block_id):
    frame_count, spatial, width = query.shape
    reach_count = window.shape[0]
    heads = bias_table.shape[1]
    head_size = width // heads
    split = window.reshape(reach_count, frame_count, spatial, 2, heads, head_size)
    keys = split[:, :, :, 0].astype(jnp.float32)
    values = split[:, :, :, 1].astype(jnp.float32)
    queries_h = query.reshape(frame_count, spatial, heads, head_size).astype(jnp.float32)
    dots = jnp.einsum('fshd,mgshd->shfmg', queries_h, keys)
    bias, query_pos, reach_pos, key_pos = bias_terms(bucket_table, bias_table, frame_count, reach_count)
    allowed = ((reach_pos > 0) | (key_pos <= query_pos)) & ((mask_row[None, :, None] == 1) | (reach_pos == 0)) & (block_id - reach_pos >= 0)
    scores = dots * (head_size ** -0.5) + bias[None]
    scores = jnp.where(allowed[None, None], scores, -1e30)
    top = jnp.max(scores, axis=(3, 4), keepdims=True)
    expo = jnp.exp(scores - top)
    weights = (expo / jnp.sum(expo, axis=(3, 4), keepdims=True)).astype(jnp.bfloat16)
    mixed = jnp.einsum('shfmg,mgshd->fshd', weights.astype(jnp.float32), values)
    return mixed.astype(jnp.bfloat16).reshape(frame_count, spatial, width)


def to_blocks(array):
    groups, cycle_frames, spatial, width = array.shape
    shaped = array.reshape(N_OUTER, N_INNER, FR_DEV, spatial, width)
    return jnp.transpose(shaped, (1, 0, 2, 3, 4)).reshape(N_INNER * N_OUTER, FR_DEV, spatial, width)


def reference(frames, queries, w_keyval, bucket_table, bias_table, block_mask):
    groups, cycle_frames, spatial, width = frames.shape
    blocks = N_INNER * N_OUTER
    keyval = jnp.dot(frames.reshape(-1, width), w_keyval, preferred_element_type=jnp.float32).astype(jnp.bfloat16)
    keyval = to_blocks(keyval.reshape(groups, cycle_frames, spatial, -1))
    padding = jnp.zeros((SPAN,) + keyval.shape[1:], jnp.bfloat16)
    padded = jnp.concatenate([padding, keyval], axis=0)
    query_blocks = to_blocks(queries)
    masks = jnp.transpose(block_mask, (1, 0, 2)).reshape(blocks, SPAN + 1)

    def one_block(block_id):
        window = lax.dynamic_slice_in_dim(padded, block_id, SPAN + 1, 0)[::-1]
        return attend(query_blocks[block_id], window, bucket_table, bias_table, masks[block_id], block_id)

    result = lax.map(one_block, jnp.arange(blocks, dtype=jnp.int32))
    shaped = result.reshape(N_INNER, N_OUTER, FR_DEV, spatial, queries.shape[3])
    return jnp.transpose(shaped, (1, 0, 2, 3, 4)).reshape(queries.shape)
```

```python
import jax
import jax.numpy as jnp
from jax import lax
from jax.experimental import pallas as pl
from jax.experimental.pallas import tpu as pltpu
from jax.sharding import PartitionSpec as P

SPAN = 8
HEAD = 128
HEADS = 8
ROWS = 8
GROUP = 64
FR = 6
CHUNK = SPAN * FR
KEYS = 128
NEG = -1e30
VMEM = pl.BlockSpec(memory_space=pltpu.VMEM)
SMEM = pl.BlockSpec(memory_space=pltpu.SMEM)


def swap_matrix(frames, rows, back):
    size = frames * rows
    a = lax.broadcasted_iota(jnp.int32, (size, size), 1 if back else 0)
    b = lax.broadcasted_iota(jnp.int32, (size, size), 0 if back else 1)
    hit = b == (a % frames) * rows + a // frames
    return jnp.where(hit, 1.0, 0.0).astype(jnp.bfloat16)


def prep_kernel(head_ref, bucket_ref, table_ref, x_ref, wk_ref, wv_ref, q_ref, out_ref, base_ref):
    step = pl.program_id(0)
    w = jnp.concatenate([wk_ref[...], wv_ref[...]], axis=1)
    kv = jnp.dot(x_ref[...], w, preferred_element_type=jnp.float32)
    q = q_ref[...].astype(jnp.float32)
    spatial = x_ref.shape[0] // FR
    for group in range(spatial // ROWS):
        at = [f * spatial + group * ROWS for f in range(FR)]
        both = jnp.concatenate([kv[a : a + ROWS] for a in at], axis=0)
        mine = jnp.concatenate([q[a : a + ROWS] for a in at], axis=0)
        out_ref[group, 0, :, 0 : 2 * HEAD] = both.astype(jnp.bfloat16)
        out_ref[group, 0, :, 2 * HEAD :] = mine.astype(jnp.bfloat16)

    @pl.when(step == 0)
    def _():
        head = head_ref[0]
        i = lax.broadcasted_iota(jnp.int32, (CHUNK, KEYS), 0)
        key = lax.broadcasted_iota(jnp.int32, (CHUNK, KEYS), 1) - (KEYS - CHUNK)
        off = i - key
        bias = jnp.full((CHUNK, KEYS), NEG, jnp.float32)
        for d in range(bucket_ref.shape[0]):
            bias = jnp.where(off == d, table_ref[bucket_ref[d], head], bias)
        reach = i // FR - (key + 96 * FR) // FR + 96
        base_ref[...] = jnp.where((reach >= 0) & (reach <= SPAN), bias, NEG)


def prep(frames, queries, w_keyval, bucket_table, bias_table, head):
    tokens, width = frames.shape
    groups = tokens // FR // ROWS
    return pl.pallas_call(
        prep_kernel,
        grid=(HEADS,),
        in_specs=[
            SMEM,
            SMEM,
            SMEM,
            pl.BlockSpec((tokens, width), lambda h: (0, 0)),
            pl.BlockSpec((width, HEAD), lambda h: (0, h)),
            pl.BlockSpec((width, HEAD), lambda h: (0, h + HEADS)),
            pl.BlockSpec((tokens, HEAD), lambda h: (0, h)),
        ],
        out_specs=[
            pl.BlockSpec((groups, 1, CHUNK, 3 * HEAD), lambda h: (0, h, 0, 0)),
            pl.BlockSpec((CHUNK, KEYS), lambda h: (0, 0)),
        ],
        out_shape=[
            jax.ShapeDtypeStruct((groups, HEADS, CHUNK, 3 * HEAD), jnp.bfloat16),
            jax.ShapeDtypeStruct((CHUNK, KEYS), jnp.float32),
        ],
        compiler_params=pltpu.CompilerParams(vmem_limit_bytes=40 * 1024 * 1024),
        name="prep",
    )(head, bucket_table, bias_table, frames, w_keyval, w_keyval, queries)


def chunk_bias(base, rows):
    i = lax.broadcasted_iota(jnp.int32, (CHUNK, SPAN), 0)
    b = lax.broadcasted_iota(jnp.int32, (CHUNK, SPAN), 1)
    spread = jnp.where(i // FR == b, 1.0, 0.0).astype(jnp.bfloat16)
    seen = jnp.dot(spread, rows.astype(jnp.bfloat16), preferred_element_type=jnp.float32)
    return jnp.where(seen > 0.5, base, NEG)


def attend(q, k, v, bias):
    scores = lax.dot_general(q, k, (((1,), (1,)), ((), ())), preferred_element_type=jnp.float32)
    scores = scores * (HEAD**-0.5) + bias
    expo = jnp.exp(scores - jnp.max(scores, axis=1, keepdims=True))
    weights = expo * (1.0 / jnp.sum(expo, axis=1, keepdims=True))
    return jnp.dot(weights.astype(jnp.bfloat16), v, preferred_element_type=jnp.float32)


PIECE = 16


def main_kernel(base_ref, seen_ref, got_ref, out_ref, held, mixed):
    swap = swap_matrix(PIECE, ROWS, False)
    back = swap_matrix(PIECE, ROWS, True)
    frames = GROUP * FR
    lead = CHUNK
    held[:, 0:lead, :] = jnp.zeros((ROWS, lead, 3 * HEAD), jnp.bfloat16)
    for piece in range(frames // PIECE):
        rows = got_ref[piece * PIECE * ROWS : (piece + 1) * PIECE * ROWS, :]
        turned = jnp.dot(swap, rows, preferred_element_type=jnp.float32).astype(jnp.bfloat16)
        at = lead + piece * PIECE
        held[:, at : at + PIECE, :] = turned.reshape(ROWS, PIECE, 3 * HEAD)
    for chunk in range(1, GROUP // SPAN):
        bias = chunk_bias(base_ref[...], seen_ref[chunk * SPAN : (chunk + 1) * SPAN, :])
        start = lead + chunk * CHUNK
        first = start + CHUNK - KEYS
        for s in range(ROWS):
            mixed[s, chunk * CHUNK : (chunk + 1) * CHUNK, :] = attend(
                held[s, start : start + CHUNK, 2 * HEAD :],
                held[s, first : first + KEYS, 0:HEAD],
                held[s, first : first + KEYS, HEAD : 2 * HEAD],
                bias,
            ).astype(jnp.bfloat16)
    for piece in range(CHUNK // PIECE, frames // PIECE):
        rows = mixed[:, piece * PIECE : (piece + 1) * PIECE, :].reshape(PIECE * ROWS, HEAD)
        out_ref[piece * PIECE * ROWS : (piece + 1) * PIECE * ROWS, :] = jnp.dot(
            back, rows, preferred_element_type=jnp.float32
        ).astype(jnp.bfloat16)


def main_part(base, seen, got):
    frames = GROUP * FR
    return pl.pallas_call(
        main_kernel,
        in_specs=[VMEM] * 3,
        out_specs=VMEM,
        out_shape=jax.ShapeDtypeStruct((frames * ROWS, HEAD), jnp.bfloat16),
        scratch_shapes=[
            pltpu.VMEM((ROWS, CHUNK + frames, 3 * HEAD), jnp.bfloat16),
            pltpu.VMEM((ROWS, frames, HEAD), jnp.bfloat16),
        ],
        compiler_params=pltpu.CompilerParams(vmem_limit_bytes=40 * 1024 * 1024),
        cost_estimate=pl.CostEstimate(flops=2_000_000_000, bytes_accessed=16_000_000, transcendentals=0),
        name="main_part",
    )(base, seen, got)


def first_kernel(base_ref, seen_ref, got_ref, halo_ref, rest_ref, out_ref, held, mixed):
    swap = swap_matrix(PIECE, ROWS, False)
    back = swap_matrix(PIECE, ROWS, True)
    lead = KEYS - 2 * CHUNK
    held[:, 0:lead, :] = jnp.zeros((ROWS, lead, 3 * HEAD), jnp.bfloat16)
    for piece in range(CHUNK // PIECE):
        span = slice(piece * PIECE * ROWS, (piece + 1) * PIECE * ROWS)
        turned = jnp.dot(swap, halo_ref[span, :], preferred_element_type=jnp.float32)
        at = lead + piece * PIECE
        held[:, at : at + PIECE, 0 : 2 * HEAD] = turned.astype(jnp.bfloat16).reshape(ROWS, PIECE, 2 * HEAD)
        turned = jnp.dot(swap, got_ref[span, :], preferred_element_type=jnp.float32)
        at = lead + CHUNK + piece * PIECE
        held[:, at : at + PIECE, :] = turned.astype(jnp.bfloat16).reshape(ROWS, PIECE, 3 * HEAD)
    bias = chunk_bias(base_ref[...], seen_ref[0:SPAN, :])
    for s in range(ROWS):
        mixed[s] = attend(
            held[s, KEYS - CHUNK : KEYS, 2 * HEAD :],
            held[s, :, 0:HEAD],
            held[s, :, HEAD : 2 * HEAD],
            bias,
        ).astype(jnp.bfloat16)
    for piece in range(CHUNK // PIECE):
        rows = mixed[:, piece * PIECE : (piece + 1) * PIECE, :].reshape(PIECE * ROWS, HEAD)
        out_ref[piece * PIECE * ROWS : (piece + 1) * PIECE * ROWS, :] = jnp.dot(
            back, rows, preferred_element_type=jnp.float32
        ).astype(jnp.bfloat16)


def first_part(base, seen, got, halo, rest):
    return pl.pallas_call(
        first_kernel,
        in_specs=[VMEM] * 5,
        out_specs=VMEM,
        out_shape=jax.ShapeDtypeStruct(rest.shape, rest.dtype),
        scratch_shapes=[
            pltpu.VMEM((ROWS, KEYS, 3 * HEAD), jnp.bfloat16),
            pltpu.VMEM((ROWS, CHUNK, HEAD), jnp.bfloat16),
        ],
        input_output_aliases={4: 0},
        compiler_params=pltpu.CompilerParams(vmem_limit_bytes=40 * 1024 * 1024),
        name="first_part",
    )(base, seen, got, halo, rest)


def exchange(array, groups):
    return lax.all_to_all(array, ("inner", "outer"), 0, 0, tiled=True, axis_index_groups=groups)


def on_device(frames, queries, w_keyval, bucket_table, bias_table, block_mask):
    n_outer = lax.axis_size("outer")
    n_blocks = lax.axis_size("inner") * n_outer
    block = lax.axis_index("inner") * n_outer + lax.axis_index("outer")
    groups = [list(range(g, g + GROUP)) for g in range(0, n_blocks, GROUP)]
    spatial, width = frames.shape[2:]

    frame = jnp.arange(KEYS, dtype=jnp.int32) - (KEYS - CHUNK)
    reach = block % SPAN - (frame + 96 * FR) // FR + 96
    mask = block_mask.reshape(-1)
    steps = jnp.arange(SPAN + 1, dtype=jnp.int32)
    allowed = ((mask == 1) | (steps == 0)) & (block - steps >= 0)
    hit = (reach[:, None] == steps[None, :]) & allowed[None, :]
    seen = jnp.max(hit.astype(jnp.float32), axis=1)[None, :]
    seen = lax.all_gather(seen, ("inner", "outer"), axis=0, tiled=True, axis_index_groups=groups)

    head = (block % HEADS).astype(jnp.int32).reshape(1)
    sent, base = prep(
        frames.reshape(-1, width),
        queries.reshape(-1, queries.shape[3]),
        w_keyval,
        bucket_table,
        bias_table,
        head,
    )
    got = exchange(sent.reshape(GROUP, CHUNK, 3 * HEAD), groups)
    halo = got[GROUP - SPAN :, :, : 2 * HEAD].reshape(-1, 2 * HEAD)
    perm = [(i, (i + GROUP) % n_blocks) for i in range(n_blocks)]
    halo = lax.ppermute(halo, ("inner", "outer"), perm)
    got = got.reshape(-1, 3 * HEAD)
    rest = main_part(base, seen, got)
    mixed = first_part(base, seen, got, halo, rest)
    out = exchange(mixed.reshape(GROUP, CHUNK, HEAD), groups)
    out = out.reshape(spatial // ROWS, HEADS, FR, ROWS, HEAD)
    return out.transpose(2, 0, 3, 1, 4).reshape(queries.shape)


def solution(mesh):
    in_specs = (
        P("outer", "inner", None, None),
        P("outer", "inner", None, None),
        P(),
        P(),
        P(),
        P("outer", "inner", None),
    )
    out_specs = P("outer", "inner", None, None)
    return jax.shard_map(
        on_device, mesh=mesh, in_specs=in_specs, out_specs=out_specs, check_vma=False
    )
```

```python
import jax
import jax.numpy as jnp
from jax import lax
from jax.experimental import pallas as pl
from jax.experimental.pallas import tpu as pltpu
from jax.sharding import PartitionSpec as P

SPAN = 8
HEAD = 128
HEADS = 8
ROWS = 8
GROUP = 64
FR = 6
CHUNK = SPAN * FR
KEYS = 128
MESSAGE = 3 * CHUNK + ROWS
PIECE = 16
NEG = -1e30
VMEM = pl.BlockSpec(memory_space=pltpu.VMEM)
SMEM = pl.BlockSpec(memory_space=pltpu.SMEM)


def swap_matrix(frames, rows, back):
    size = frames * rows
    a = lax.broadcasted_iota(jnp.int32, (size, size), 1 if back else 0)
    b = lax.broadcasted_iota(jnp.int32, (size, size), 0 if back else 1)
    hit = b == (a % frames) * rows + a // frames
    return jnp.where(hit, 1.0, 0.0).astype(jnp.bfloat16)


def prep_kernel(place_ref, mask_ref, bucket_ref, table_ref, x_ref, wk_ref, wv_ref, q_ref, out_ref, base_ref):
    step = pl.program_id(0)
    block = place_ref[0]
    head = place_ref[1]
    spatial = x_ref.shape[0] // FR
    x = x_ref[...]
    parts = [
        jnp.dot(x, wk_ref[...], preferred_element_type=jnp.float32),
        jnp.dot(x, wv_ref[...], preferred_element_type=jnp.float32),
        q_ref[...].astype(jnp.float32),
    ]
    key = lax.broadcasted_iota(jnp.int32, (2 * ROWS, KEYS), 1) - (KEYS - CHUNK)
    reach = block % SPAN - (key + 96 * FR) // FR + 96
    seen = jnp.where(reach == 0, 1.0, 0.0)
    for m in range(1, SPAN + 1):
        open_ = jnp.where((mask_ref[m] == 1) & (block >= m), 1.0, 0.0)
        seen = jnp.where(reach == m, open_, seen)
    seen = seen.astype(jnp.bfloat16)[0:ROWS]
    for pair in range(2):
        cols = slice(pair * HEAD, (pair + 1) * HEAD)
        for group in range(spatial // ROWS):
            at = [f * spatial + group * ROWS for f in range(FR)]
            for n, part in enumerate(parts):
                rows = jnp.concatenate([part[a : a + ROWS, cols] for a in at], axis=0)
                out_ref[group, pair, n * CHUNK : (n + 1) * CHUNK, :] = rows.astype(jnp.bfloat16)
            out_ref[group, pair, 3 * CHUNK :, :] = seen

    @pl.when(step == 0)
    def _():
        i = lax.broadcasted_iota(jnp.int32, (CHUNK, KEYS), 0)
        key = lax.broadcasted_iota(jnp.int32, (CHUNK, KEYS), 1) - (KEYS - CHUNK)
        off = i - key
        bias = jnp.full((CHUNK, KEYS), NEG, jnp.float32)
        for d in range(bucket_ref.shape[0]):
            bias = jnp.where(off == d, table_ref[head, bucket_ref[d]], bias)
        reach = i // FR - (key + 96 * FR) // FR + 96
        base_ref[...] = jnp.where((reach >= 0) & (reach <= SPAN), bias, NEG)


def prep(frames, queries, w_keyval, bucket_table, bias_table, block_mask, place):
    tokens, width = frames.shape
    groups = tokens // FR // ROWS
    half = HEADS // 2
    return pl.pallas_call(
        prep_kernel,
        grid=(half,),
        in_specs=[
            SMEM,
            SMEM,
            SMEM,
            SMEM,
            pl.BlockSpec((tokens, width), lambda h: (0, 0)),
            pl.BlockSpec((width, 2 * HEAD), lambda h: (0, h)),
            pl.BlockSpec((width, 2 * HEAD), lambda h: (0, h + half)),
            pl.BlockSpec((tokens, 2 * HEAD), lambda h: (0, h)),
        ],
        out_specs=[
            pl.BlockSpec((groups, 2, MESSAGE, HEAD), lambda h: (0, h, 0, 0)),
            pl.BlockSpec((CHUNK, KEYS), lambda h: (0, 0)),
        ],
        out_shape=[
            jax.ShapeDtypeStruct((groups, HEADS, MESSAGE, HEAD), jnp.bfloat16),
            jax.ShapeDtypeStruct((CHUNK, KEYS), jnp.float32),
        ],
        compiler_params=pltpu.CompilerParams(vmem_limit_bytes=60 * 1024 * 1024),
        name="prep",
    )(place, block_mask, bucket_table, bias_table, frames, w_keyval, w_keyval, queries)


def chunk_bias(base, rows):
    i = lax.broadcasted_iota(jnp.int32, (CHUNK, SPAN * ROWS), 0)
    b = lax.broadcasted_iota(jnp.int32, (CHUNK, SPAN * ROWS), 1)
    spread = jnp.where(i // FR * ROWS == b, 1.0, 0.0).astype(jnp.bfloat16)
    rows = rows.astype(jnp.float32).reshape(SPAN * ROWS, KEYS).astype(jnp.bfloat16)
    seen = jnp.dot(spread, rows, preferred_element_type=jnp.float32)
    return jnp.where(seen > 0.5, base, NEG)


def attend(held, start, bias):
    first = start + CHUNK - KEYS
    scores = [
        lax.dot_general(
            held[s, start : start + CHUNK, 2 * HEAD :],
            held[s, first : first + KEYS, 0:HEAD],
            (((1,), (1,)), ((), ())),
            preferred_element_type=jnp.float32,
        )
        for s in range(ROWS)
    ]
    scores = jnp.stack(scores, axis=0) * (HEAD**-0.5) + bias[None]
    expo = jnp.exp(scores - jnp.max(scores, axis=2, keepdims=True))
    weights = expo * (1.0 / jnp.sum(expo, axis=2, keepdims=True))
    weights = weights.astype(jnp.bfloat16)
    return [
        jnp.dot(
            weights[s], held[s, first : first + KEYS, HEAD : 2 * HEAD], preferred_element_type=jnp.float32
        ).astype(jnp.bfloat16)
        for s in range(ROWS)
    ]


def turn_in(held, swap, got_ref, blocks, parts, at):
    rows = [
        got_ref[blocks, n * CHUNK : (n + 1) * CHUNK, :].reshape(CHUNK * ROWS, HEAD) for n in range(parts)
    ]
    rows = jnp.concatenate(rows, axis=1)
    for piece in range(CHUNK // PIECE):
        part = rows[piece * PIECE * ROWS : (piece + 1) * PIECE * ROWS]
        turned = jnp.dot(swap, part, preferred_element_type=jnp.float32).astype(jnp.bfloat16)
        start = at + piece * PIECE
        held[:, start : start + PIECE, 0 : parts * HEAD] = turned.reshape(ROWS, PIECE, parts * HEAD)


def turn_out(out_ref, back, mixed, at):
    for piece in range(CHUNK // PIECE):
        rows = [m[piece * PIECE : (piece + 1) * PIECE] for m in mixed]
        rows = jnp.concatenate(rows, axis=0)
        start = at + piece * PIECE * ROWS
        out_ref[start : start + PIECE * ROWS, :] = jnp.dot(
            back, rows, preferred_element_type=jnp.float32
        ).astype(jnp.bfloat16)


def main_kernel(base_ref, got_ref, out_ref, held):
    swap = swap_matrix(PIECE, ROWS, False)
    back = swap_matrix(PIECE, ROWS, True)
    lead = CHUNK
    held[:, 0:lead, :] = jnp.zeros((ROWS, lead, 3 * HEAD), jnp.bfloat16)
    for chunk in range(GROUP // SPAN):
        blocks = slice(chunk * SPAN, (chunk + 1) * SPAN)
        at = lead + chunk * CHUNK
        turn_in(held, swap, got_ref, blocks, 3, at)
        if chunk > 0:
            bias = chunk_bias(base_ref[...], got_ref[blocks, 3 * CHUNK :, :])
            turn_out(out_ref, back, attend(held, at, bias), chunk * CHUNK * ROWS)


def main_part(base, got):
    frames = GROUP * FR
    return pl.pallas_call(
        main_kernel,
        in_specs=[VMEM] * 2,
        out_specs=VMEM,
        out_shape=jax.ShapeDtypeStruct((frames * ROWS, HEAD), jnp.bfloat16),
        scratch_shapes=[pltpu.VMEM((ROWS, CHUNK + frames, 3 * HEAD), jnp.bfloat16)],
        compiler_params=pltpu.CompilerParams(vmem_limit_bytes=40 * 1024 * 1024),
        cost_estimate=pl.CostEstimate(flops=2_000_000_000, bytes_accessed=16_000_000, transcendentals=0),
        name="main_part",
    )(base, got)


def first_kernel(base_ref, got_ref, halo_ref, rest_ref, out_ref, held):
    swap = swap_matrix(PIECE, ROWS, False)
    back = swap_matrix(PIECE, ROWS, True)
    lead = KEYS - 2 * CHUNK
    blocks = slice(0, SPAN)
    held[:, 0:lead, :] = jnp.zeros((ROWS, lead, 3 * HEAD), jnp.bfloat16)
    turn_in(held, swap, halo_ref, blocks, 2, lead)
    turn_in(held, swap, got_ref, blocks, 3, lead + CHUNK)
    bias = chunk_bias(base_ref[...], got_ref[blocks, 3 * CHUNK :, :])
    turn_out(out_ref, back, attend(held, lead + CHUNK, bias), 0)


def first_part(base, got, halo, rest):
    return pl.pallas_call(
        first_kernel,
        in_specs=[VMEM] * 4,
        out_specs=VMEM,
        out_shape=jax.ShapeDtypeStruct(rest.shape, rest.dtype),
        scratch_shapes=[pltpu.VMEM((ROWS, KEYS, 3 * HEAD), jnp.bfloat16)],
        input_output_aliases={3: 0},
        compiler_params=pltpu.CompilerParams(vmem_limit_bytes=40 * 1024 * 1024),
        name="first_part",
    )(base, got, halo, rest)


def exchange(array, groups):
    return lax.all_to_all(array, ("inner", "outer"), 0, 0, tiled=True, axis_index_groups=groups)


def on_device(frames, queries, w_keyval, bucket_table, bias_table, block_mask):
    n_outer = lax.axis_size("outer")
    n_blocks = lax.axis_size("inner") * n_outer
    block = lax.axis_index("inner") * n_outer + lax.axis_index("outer")
    groups = [list(range(g, g + GROUP)) for g in range(0, n_blocks, GROUP)]
    spatial, width = frames.shape[2:]

    place = jnp.stack([block, block % HEADS]).astype(jnp.int32)
    sent, base = prep(
        frames.reshape(-1, width),
        queries.reshape(-1, queries.shape[3]),
        w_keyval,
        bucket_table,
        bias_table.T,
        block_mask.reshape(-1),
        place,
    )
    got = exchange(sent.reshape(GROUP, MESSAGE, HEAD), groups)
    perm = [(i, (i + GROUP) % n_blocks) for i in range(n_blocks)]
    halo = lax.ppermute(got[GROUP - SPAN :, : 2 * CHUNK, :], ("inner", "outer"), perm)
    rest = main_part(base, got)
    mixed = first_part(base, got, halo, rest)
    out = exchange(mixed.reshape(GROUP, CHUNK, HEAD), groups)
    out = out.reshape(spatial // ROWS, HEADS, FR, ROWS, HEAD)
    return out.transpose(2, 0, 3, 1, 4).reshape(queries.shape)


def solution(mesh):
    in_specs = (
        P("outer", "inner", None, None),
        P("outer", "inner", None, None),
        P(),
        P(),
        P(),
        P("outer", "inner", None),
    )
    out_specs = P("outer", "inner", None, None)
    return jax.shard_map(
        on_device, mesh=mesh, in_specs=in_specs, out_specs=out_specs, check_vma=False
    )
```

```python
import jax
import jax.numpy as jnp
from jax import lax
from jax.experimental import pallas as pl
from jax.experimental.pallas import tpu as pltpu
from jax.sharding import PartitionSpec as P

SPAN = 8
HEAD = 128
HEADS = 8
ROWS = 8
GROUP = 64
FR = 6
CHUNK = SPAN * FR
KEYS = 128
MESSAGE = 3 * CHUNK + ROWS
PIECE = 16
SLABS = 4
NEG = -1e30
VMEM = pl.BlockSpec(memory_space=pltpu.VMEM)
SMEM = pl.BlockSpec(memory_space=pltpu.SMEM)


def swap_matrix(frames, rows, back):
    size = frames * rows
    a = lax.broadcasted_iota(jnp.int32, (size, size), 1 if back else 0)
    b = lax.broadcasted_iota(jnp.int32, (size, size), 0 if back else 1)
    hit = b == (a % frames) * rows + a // frames
    return jnp.where(hit, 1.0, 0.0).astype(jnp.bfloat16)


def block_number():
    return lax.axis_index("inner") * lax.axis_size("outer") + lax.axis_index("outer")


def prep_kernel(mask_ref, x_hbm, w_hbm, q_hbm, out_hbm, x, w, q, total, out_ref, x_sem, w_sem, q_sem, out_sem):
    depth = w.shape[0] // SLABS
    loads = []
    for slab in range(SLABS):
        span = slice(slab * depth, (slab + 1) * depth)
        loads.append(
            (
                pltpu.make_async_copy(x_hbm.at[:, span], x.at[:, span], x_sem.at[slab]),
                pltpu.make_async_copy(w_hbm.at[span], w.at[span], w_sem.at[slab]),
            )
        )
    q_load = pltpu.make_async_copy(q_hbm, q, q_sem)
    for load in loads[0] + loads[1]:
        load.start()
    spatial = x.shape[0] // FR

    def place(part, pair, n):
        for half in range(2):
            cols = slice(half * HEAD, (half + 1) * HEAD)
            for group in range(spatial // ROWS):
                at = [f * spatial + group * ROWS for f in range(FR)]
                rows = jnp.concatenate([part[a : a + ROWS, cols] for a in at], axis=0)
                out_ref[group, 2 * pair + half, n * CHUNK : (n + 1) * CHUNK, :] = rows.astype(jnp.bfloat16)

    block = block_number()
    key = lax.broadcasted_iota(jnp.int32, (2 * ROWS, KEYS), 1) - (KEYS - CHUNK)
    reach = block % SPAN - (key + 96 * FR) // FR + 96
    seen = jnp.where(reach == 0, 1.0, 0.0)
    for m in range(1, SPAN + 1):
        visible = jnp.where((mask_ref[m] == 1) & (block >= m), 1.0, 0.0)
        seen = jnp.where(reach == m, visible, seen)
    seen = seen.astype(jnp.bfloat16)[0:ROWS]
    for group in range(spatial // ROWS):
        for head in range(HEADS):
            out_ref[group, head, 3 * CHUNK :, :] = seen

    for slab in range(SLABS):
        for load in loads[slab]:
            load.wait()
        if slab + 2 < SLABS:
            for load in loads[slab + 2]:
                load.start()
        if slab == 0:
            q_load.start()
        if slab == SLABS - 1:
            q_load.wait()
            for pair in range(HEADS // 2):
                place(q[:, pair * 2 * HEAD : (pair + 1) * 2 * HEAD].astype(jnp.float32), pair, 2)
        span = slice(slab * depth, (slab + 1) * depth)
        stores = []
        for pair in range(HEADS // 2):
            for n in range(2):
                first = (n * HEADS + 2 * pair) * HEAD
                cols = slice(first, first + 2 * HEAD)
                part = jnp.dot(x[:, span], w[span, cols], preferred_element_type=jnp.float32)
                if slab > 0:
                    part = part + total[:, cols]
                if slab < SLABS - 1:
                    total[:, cols] = part
                else:
                    place(part, pair, n)
            if slab == SLABS - 1:
                heads = slice(2 * pair, 2 * pair + 2)
                store = pltpu.make_async_copy(out_ref.at[:, heads], out_hbm.at[:, heads], out_sem.at[pair])
                store.start()
                stores.append(store)
    for store in stores:
        store.wait()


def prep(frames, queries, w_keyval, block_mask):
    tokens, width = frames.shape
    groups = tokens // FR // ROWS
    any_ = pl.BlockSpec(memory_space=pl.ANY)
    return pl.pallas_call(
        prep_kernel,
        in_specs=[SMEM, any_, any_, any_],
        out_specs=any_,
        out_shape=jax.ShapeDtypeStruct((groups, HEADS, MESSAGE, HEAD), jnp.bfloat16),
        scratch_shapes=[
            pltpu.VMEM(frames.shape, jnp.bfloat16),
            pltpu.VMEM(w_keyval.shape, jnp.bfloat16),
            pltpu.VMEM(queries.shape, jnp.bfloat16),
            pltpu.VMEM((tokens, w_keyval.shape[1]), jnp.float32),
            pltpu.VMEM((groups, HEADS, MESSAGE, HEAD), jnp.bfloat16),
            pltpu.SemaphoreType.DMA((SLABS,)),
            pltpu.SemaphoreType.DMA((SLABS,)),
            pltpu.SemaphoreType.DMA,
            pltpu.SemaphoreType.DMA((HEADS // 2,)),
        ],
        compiler_params=pltpu.CompilerParams(vmem_limit_bytes=58 * 1024 * 1024),
        name="prep",
    )(block_mask, frames, w_keyval, queries)


def bias_of_head(bucket_ref, table_ref):
    head = block_number() % HEADS
    i = lax.broadcasted_iota(jnp.int32, (CHUNK, KEYS), 0)
    key = lax.broadcasted_iota(jnp.int32, (CHUNK, KEYS), 1) - (KEYS - CHUNK)
    off = i - key
    bias = jnp.full((CHUNK, KEYS), NEG, jnp.float32)
    for d in range(bucket_ref.shape[0]):
        bias = jnp.where(off == d, table_ref[head, bucket_ref[d]], bias)
    reach = i // FR - (key + 96 * FR) // FR + 96
    return jnp.where((reach >= 0) & (reach <= SPAN), bias, NEG)


def chunk_bias(base, rows):
    i = lax.broadcasted_iota(jnp.int32, (CHUNK, SPAN * ROWS), 0)
    b = lax.broadcasted_iota(jnp.int32, (CHUNK, SPAN * ROWS), 1)
    spread = jnp.where(i // FR * ROWS == b, 1.0, 0.0).astype(jnp.bfloat16)
    rows = rows.astype(jnp.float32).reshape(SPAN * ROWS, KEYS).astype(jnp.bfloat16)
    seen = jnp.dot(spread, rows, preferred_element_type=jnp.float32)
    return jnp.where(seen > 0.5, base, NEG)


def attend(held, start, bias):
    first = start + CHUNK - KEYS
    scores = [
        lax.dot_general(
            held[s, start : start + CHUNK, 2 * HEAD :],
            held[s, first : first + KEYS, 0:HEAD],
            (((1,), (1,)), ((), ())),
            preferred_element_type=jnp.float32,
        )
        for s in range(ROWS)
    ]
    scores = jnp.stack(scores, axis=0) * (HEAD**-0.5) + bias[None]
    expo = jnp.exp(scores - jnp.max(scores, axis=2, keepdims=True))
    weights = expo * (1.0 / jnp.sum(expo, axis=2, keepdims=True))
    weights = weights.astype(jnp.bfloat16)
    return [
        jnp.dot(
            weights[s], held[s, first : first + KEYS, HEAD : 2 * HEAD], preferred_element_type=jnp.float32
        ).astype(jnp.bfloat16)
        for s in range(ROWS)
    ]


def turn_in(held, swap, got_ref, blocks, parts, at):
    rows = [
        got_ref[blocks, n * CHUNK : (n + 1) * CHUNK, :].reshape(CHUNK * ROWS, HEAD) for n in range(parts)
    ]
    rows = jnp.concatenate(rows, axis=1)
    for piece in range(CHUNK // PIECE):
        part = rows[piece * PIECE * ROWS : (piece + 1) * PIECE * ROWS]
        turned = jnp.dot(swap, part, preferred_element_type=jnp.float32).astype(jnp.bfloat16)
        start = at + piece * PIECE
        held[:, start : start + PIECE, 0 : parts * HEAD] = turned.reshape(ROWS, PIECE, parts * HEAD)


def turn_out(out_ref, back, mixed, at):
    for piece in range(CHUNK // PIECE):
        rows = [m[piece * PIECE : (piece + 1) * PIECE] for m in mixed]
        rows = jnp.concatenate(rows, axis=0)
        start = at + piece * PIECE * ROWS
        out_ref[start : start + PIECE * ROWS, :] = jnp.dot(
            back, rows, preferred_element_type=jnp.float32
        ).astype(jnp.bfloat16)


def main_kernel(bucket_ref, table_ref, got_ref, out_ref, base_ref, held):
    base_ref[...] = bias_of_head(bucket_ref, table_ref)
    swap = swap_matrix(PIECE, ROWS, False)
    back = swap_matrix(PIECE, ROWS, True)
    lead = CHUNK
    held[:, 0:lead, :] = jnp.zeros((ROWS, lead, 3 * HEAD), jnp.bfloat16)
    for chunk in range(GROUP // SPAN):
        blocks = slice(chunk * SPAN, (chunk + 1) * SPAN)
        at = lead + chunk * CHUNK
        turn_in(held, swap, got_ref, blocks, 3, at)
        if chunk > 0:
            bias = chunk_bias(base_ref[...], got_ref[blocks, 3 * CHUNK :, :])
            turn_out(out_ref, back, attend(held, at, bias), chunk * CHUNK * ROWS)


def main_part(bucket_table, bias_table, got):
    frames = GROUP * FR
    return pl.pallas_call(
        main_kernel,
        in_specs=[SMEM, SMEM, VMEM],
        out_specs=[VMEM, VMEM],
        out_shape=[
            jax.ShapeDtypeStruct((frames * ROWS, HEAD), jnp.bfloat16),
            jax.ShapeDtypeStruct((CHUNK, KEYS), jnp.float32),
        ],
        scratch_shapes=[pltpu.VMEM((ROWS, CHUNK + frames, 3 * HEAD), jnp.bfloat16)],
        compiler_params=pltpu.CompilerParams(vmem_limit_bytes=40 * 1024 * 1024),
        cost_estimate=pl.CostEstimate(flops=2_000_000_000, bytes_accessed=16_000_000, transcendentals=0),
        name="main_part",
    )(bucket_table, bias_table, got)


def first_kernel(base_ref, got_ref, halo_ref, rest_ref, out_ref, held):
    swap = swap_matrix(PIECE, ROWS, False)
    back = swap_matrix(PIECE, ROWS, True)
    lead = KEYS - 2 * CHUNK
    blocks = slice(0, SPAN)
    held[:, 0:lead, :] = jnp.zeros((ROWS, lead, 3 * HEAD), jnp.bfloat16)
    turn_in(held, swap, halo_ref, blocks, 2, lead)
    turn_in(held, swap, got_ref, blocks, 3, lead + CHUNK)
    bias = chunk_bias(base_ref[...], got_ref[blocks, 3 * CHUNK :, :])
    turn_out(out_ref, back, attend(held, lead + CHUNK, bias), 0)


def first_part(base, got, halo, rest):
    return pl.pallas_call(
        first_kernel,
        in_specs=[VMEM] * 4,
        out_specs=VMEM,
        out_shape=jax.ShapeDtypeStruct(rest.shape, rest.dtype),
        scratch_shapes=[pltpu.VMEM((ROWS, KEYS, 3 * HEAD), jnp.bfloat16)],
        input_output_aliases={3: 0},
        compiler_params=pltpu.CompilerParams(vmem_limit_bytes=40 * 1024 * 1024),
        name="first_part",
    )(base, got, halo, rest)


def exchange(array, groups):
    return lax.all_to_all(array, ("inner", "outer"), 0, 0, tiled=True, axis_index_groups=groups)


def on_device(frames, queries, w_keyval, bucket_table, bias_table, block_mask):
    n_outer = lax.axis_size("outer")
    n_blocks = lax.axis_size("inner") * n_outer
    groups = [list(range(g, g + GROUP)) for g in range(0, n_blocks, GROUP)]
    spatial, width = frames.shape[2:]

    sent = prep(
        frames.reshape(-1, width),
        queries.reshape(-1, queries.shape[3]),
        w_keyval,
        block_mask.reshape(-1),
    )
    got = exchange(sent.reshape(GROUP, MESSAGE, HEAD), groups)
    perm = [(i, (i + GROUP) % n_blocks) for i in range(n_blocks)]
    halo = lax.ppermute(got[GROUP - SPAN :, : 2 * CHUNK, :], ("inner", "outer"), perm)
    rest, base = main_part(bucket_table, bias_table.T, got)
    mixed = first_part(base, got, halo, rest)
    out = exchange(mixed.reshape(GROUP, CHUNK, HEAD), groups)
    out = out.reshape(spatial // ROWS, HEADS, FR, ROWS, HEAD)
    return out.transpose(2, 0, 3, 1, 4).reshape(queries.shape)


def solution(mesh):
    in_specs = (
        P("outer", "inner", None, None),
        P("outer", "inner", None, None),
        P(),
        P(),
        P(),
        P("outer", "inner", None),
    )
    out_specs = P("outer", "inner", None, None)
    return jax.shard_map(
        on_device, mesh=mesh, in_specs=in_specs, out_specs=out_specs, check_vma=False
    )
```

```python
import jax
import jax.numpy as jnp
from jax import lax
from jax.experimental import pallas as pl
from jax.experimental.pallas import tpu as pltpu
from jax.sharding import PartitionSpec as P

SPAN = 8
HEAD = 128
HEADS = 8
ROWS = 8
GROUP = 64
FR = 6
CHUNK = SPAN * FR
KEYS = 128
MESSAGE = 3 * CHUNK + ROWS
PIECE = 16
SLABS = 4
NEG = -1e30
VMEM = pl.BlockSpec(memory_space=pltpu.VMEM)
SMEM = pl.BlockSpec(memory_space=pltpu.SMEM)


def swap_matrix(frames, rows, back):
    size = frames * rows
    a = lax.broadcasted_iota(jnp.int32, (size, size), 1 if back else 0)
    b = lax.broadcasted_iota(jnp.int32, (size, size), 0 if back else 1)
    hit = b == (a % frames) * rows + a // frames
    return jnp.where(hit, 1.0, 0.0).astype(jnp.bfloat16)


def block_number():
    return lax.axis_index("inner") * lax.axis_size("outer") + lax.axis_index("outer")


def prep_kernel(mask_ref, x_hbm, w_hbm, q_hbm, out_hbm, x, w, q, total, out_ref, x_sem, w_sem, q_sem, out_sem):
    depth = w.shape[0] // SLABS
    loads = []
    for slab in range(SLABS):
        span = slice(slab * depth, (slab + 1) * depth)
        loads.append(
            (
                pltpu.make_async_copy(x_hbm.at[:, span], x.at[:, span], x_sem.at[slab]),
                pltpu.make_async_copy(w_hbm.at[span], w.at[span], w_sem.at[slab]),
            )
        )
    q_load = pltpu.make_async_copy(q_hbm, q, q_sem)
    for load in loads[0] + loads[1]:
        load.start()
    spatial = x.shape[0] // FR

    def place(part, pair, n):
        for half in range(2):
            cols = slice(half * HEAD, (half + 1) * HEAD)
            for group in range(spatial // ROWS):
                at = [f * spatial + group * ROWS for f in range(FR)]
                rows = jnp.concatenate([part[a : a + ROWS, cols] for a in at], axis=0)
                out_ref[group, 2 * pair + half, n * CHUNK : (n + 1) * CHUNK, :] = rows.astype(jnp.bfloat16)

    block = block_number()
    key = lax.broadcasted_iota(jnp.int32, (2 * ROWS, KEYS), 1) - (KEYS - CHUNK)
    reach = block % SPAN - (key + 96 * FR) // FR + 96
    seen = jnp.where(reach == 0, 1.0, 0.0)
    for m in range(1, SPAN + 1):
        visible = jnp.where((mask_ref[m] == 1) & (block >= m), 1.0, 0.0)
        seen = jnp.where(reach == m, visible, seen)
    seen = seen.astype(jnp.bfloat16)[0:ROWS]
    for group in range(spatial // ROWS):
        for head in range(HEADS):
            out_ref[group, head, 3 * CHUNK :, :] = seen

    for slab in range(SLABS):
        for load in loads[slab]:
            load.wait()
        if slab + 2 < SLABS:
            for load in loads[slab + 2]:
                load.start()
        if slab == 0:
            q_load.start()
        if slab == SLABS - 1:
            q_load.wait()
            for pair in range(HEADS // 2):
                place(q[:, pair * 2 * HEAD : (pair + 1) * 2 * HEAD].astype(jnp.float32), pair, 2)
        span = slice(slab * depth, (slab + 1) * depth)
        stores = []
        for pair in range(HEADS // 2):
            for n in range(2):
                first = (n * HEADS + 2 * pair) * HEAD
                cols = slice(first, first + 2 * HEAD)
                part = jnp.dot(x[:, span], w[span, cols], preferred_element_type=jnp.float32)
                if slab > 0:
                    part = part + total[:, cols]
                if slab < SLABS - 1:
                    total[:, cols] = part
                else:
                    place(part, pair, n)
            if slab == SLABS - 1:
                heads = slice(2 * pair, 2 * pair + 2)
                store = pltpu.make_async_copy(out_ref.at[:, heads], out_hbm.at[:, heads], out_sem.at[pair])
                store.start()
                stores.append(store)
    for store in stores:
        store.wait()


def prep(frames, queries, w_keyval, block_mask):
    tokens, width = frames.shape
    groups = tokens // FR // ROWS
    any_ = pl.BlockSpec(memory_space=pl.ANY)
    return pl.pallas_call(
        prep_kernel,
        in_specs=[SMEM, any_, any_, any_],
        out_specs=any_,
        out_shape=jax.ShapeDtypeStruct((groups, HEADS, MESSAGE, HEAD), jnp.bfloat16),
        scratch_shapes=[
            pltpu.VMEM(frames.shape, jnp.bfloat16),
            pltpu.VMEM(w_keyval.shape, jnp.bfloat16),
            pltpu.VMEM(queries.shape, jnp.bfloat16),
            pltpu.VMEM((tokens, w_keyval.shape[1]), jnp.float32),
            pltpu.VMEM((groups, HEADS, MESSAGE, HEAD), jnp.bfloat16),
            pltpu.SemaphoreType.DMA((SLABS,)),
            pltpu.SemaphoreType.DMA((SLABS,)),
            pltpu.SemaphoreType.DMA,
            pltpu.SemaphoreType.DMA((HEADS // 2,)),
        ],
        compiler_params=pltpu.CompilerParams(vmem_limit_bytes=58 * 1024 * 1024),
        name="prep",
    )(block_mask, frames, w_keyval, queries)


def bias_of_head(bucket_ref, table_ref):
    head = block_number() % HEADS
    i = lax.broadcasted_iota(jnp.int32, (CHUNK, KEYS), 0)
    key = lax.broadcasted_iota(jnp.int32, (CHUNK, KEYS), 1) - (KEYS - CHUNK)
    off = i - key
    bias = jnp.full((CHUNK, KEYS), NEG, jnp.float32)
    for d in range(bucket_ref.shape[0]):
        bias = jnp.where(off == d, table_ref[head, bucket_ref[d]], bias)
    reach = i // FR - (key + 96 * FR) // FR + 96
    return jnp.where((reach >= 0) & (reach <= SPAN), bias, NEG)


def chunk_bias(base, rows):
    i = lax.broadcasted_iota(jnp.int32, (CHUNK, SPAN * ROWS), 0)
    b = lax.broadcasted_iota(jnp.int32, (CHUNK, SPAN * ROWS), 1)
    spread = jnp.where(i // FR * ROWS == b, 1.0, 0.0).astype(jnp.bfloat16)
    rows = rows.astype(jnp.float32).reshape(SPAN * ROWS, KEYS).astype(jnp.bfloat16)
    seen = jnp.dot(spread, rows, preferred_element_type=jnp.float32)
    return jnp.where(seen > 0.5, base, NEG)


def attend(held, start, bias):
    first = start + CHUNK - KEYS
    scores = [
        lax.dot_general(
            held[s, start : start + CHUNK, 2 * HEAD :],
            held[s, first : first + KEYS, 0:HEAD],
            (((1,), (1,)), ((), ())),
            preferred_element_type=jnp.float32,
        )
        for s in range(ROWS)
    ]
    scores = jnp.stack(scores, axis=0) * (HEAD**-0.5) + bias[None]
    expo = jnp.exp(scores - jnp.max(scores, axis=2, keepdims=True))
    weights = expo * (1.0 / jnp.sum(expo, axis=2, keepdims=True))
    weights = weights.astype(jnp.bfloat16)
    return [
        jnp.dot(
            weights[s], held[s, first : first + KEYS, HEAD : 2 * HEAD], preferred_element_type=jnp.float32
        ).astype(jnp.bfloat16)
        for s in range(ROWS)
    ]


def turn_in(held, swap, got_ref, blocks, parts, at):
    rows = [
        got_ref[blocks, n * CHUNK : (n + 1) * CHUNK, :].reshape(CHUNK * ROWS, HEAD) for n in range(parts)
    ]
    rows = jnp.concatenate(rows, axis=1)
    for piece in range(CHUNK // PIECE):
        part = rows[piece * PIECE * ROWS : (piece + 1) * PIECE * ROWS]
        turned = jnp.dot(swap, part, preferred_element_type=jnp.float32).astype(jnp.bfloat16)
        start = at + piece * PIECE
        held[:, start : start + PIECE, 0 : parts * HEAD] = turned.reshape(ROWS, PIECE, parts * HEAD)


def turn_out(out_ref, back, mixed, at):
    for piece in range(CHUNK // PIECE):
        rows = [m[piece * PIECE : (piece + 1) * PIECE] for m in mixed]
        rows = jnp.concatenate(rows, axis=0)
        start = at + piece * PIECE * ROWS
        out_ref[start : start + PIECE * ROWS, :] = jnp.dot(
            back, rows, preferred_element_type=jnp.float32
        ).astype(jnp.bfloat16)


def main_kernel(bucket_ref, table_ref, got_ref, out_ref, base_ref, held):
    base_ref[...] = bias_of_head(bucket_ref, table_ref)
    swap = swap_matrix(PIECE, ROWS, False)
    back = swap_matrix(PIECE, ROWS, True)
    lead = CHUNK
    held[:, 0:lead, :] = jnp.zeros((ROWS, lead, 3 * HEAD), jnp.bfloat16)
    for chunk in range(GROUP // SPAN):
        blocks = slice(chunk * SPAN, (chunk + 1) * SPAN)
        at = lead + chunk * CHUNK
        turn_in(held, swap, got_ref, blocks, 3, at)
        if chunk > 0:
            bias = chunk_bias(base_ref[...], got_ref[blocks, 3 * CHUNK :, :])
            turn_out(out_ref, back, attend(held, at, bias), chunk * CHUNK * ROWS)


def main_part(bucket_table, bias_table, got):
    frames = GROUP * FR
    return pl.pallas_call(
        main_kernel,
        in_specs=[SMEM, SMEM, VMEM],
        out_specs=[VMEM, VMEM],
        out_shape=[
            jax.ShapeDtypeStruct((frames * ROWS, HEAD), jnp.bfloat16),
            jax.ShapeDtypeStruct((CHUNK, KEYS), jnp.float32),
        ],
        scratch_shapes=[pltpu.VMEM((ROWS, CHUNK + frames, 3 * HEAD), jnp.bfloat16)],
        compiler_params=pltpu.CompilerParams(vmem_limit_bytes=40 * 1024 * 1024),
        cost_estimate=pl.CostEstimate(flops=2_000_000_000, bytes_accessed=16_000_000, transcendentals=0),
        name="main_part",
    )(bucket_table, bias_table, got)


def first_kernel(base_ref, got_ref, halo_ref, rest_ref, out_ref, held):
    swap = swap_matrix(PIECE, ROWS, False)
    back = swap_matrix(PIECE, ROWS, True)
    lead = KEYS - 2 * CHUNK
    blocks = slice(0, SPAN)
    held[:, 0:lead, :] = jnp.zeros((ROWS, lead, 3 * HEAD), jnp.bfloat16)
    turn_in(held, swap, halo_ref, blocks, 2, lead)
    turn_in(held, swap, got_ref, blocks, 3, lead + CHUNK)
    bias = chunk_bias(base_ref[...], got_ref[blocks, 3 * CHUNK :, :])
    turn_out(out_ref, back, attend(held, lead + CHUNK, bias), 0)


def first_part(base, got, halo, rest):
    return pl.pallas_call(
        first_kernel,
        in_specs=[VMEM] * 4,
        out_specs=VMEM,
        out_shape=jax.ShapeDtypeStruct(rest.shape, rest.dtype),
        scratch_shapes=[pltpu.VMEM((ROWS, KEYS, 3 * HEAD), jnp.bfloat16)],
        input_output_aliases={3: 0},
        compiler_params=pltpu.CompilerParams(vmem_limit_bytes=40 * 1024 * 1024),
        name="first_part",
    )(base, got, halo, rest)


def exchange(array, groups):
    return lax.all_to_all(array, ("inner", "outer"), 0, 0, tiled=True, axis_index_groups=groups)


def on_device(frames, queries, w_keyval, bucket_table, bias_table, block_mask):
    n_outer = lax.axis_size("outer")
    n_blocks = lax.axis_size("inner") * n_outer
    groups = [list(range(g, g + GROUP)) for g in range(0, n_blocks, GROUP)]
    spatial, width = frames.shape[2:]

    sent = prep(
        frames.reshape(-1, width),
        queries.reshape(-1, queries.shape[3]),
        w_keyval,
        block_mask.reshape(-1),
    )
    got = exchange(sent.reshape(GROUP, MESSAGE, HEAD), groups)
    perm = [(i, i + GROUP) for i in range(n_blocks - GROUP)]
    halo = lax.ppermute(got[GROUP - SPAN :, : 2 * CHUNK, :], ("inner", "outer"), perm)
    rest, base = main_part(bucket_table, bias_table.T, got)
    mixed = first_part(base, got, halo, rest)
    out = exchange(mixed.reshape(GROUP, CHUNK, HEAD), groups)
    out = out.reshape(spatial // ROWS, HEADS, FR, ROWS, HEAD)
    return out.transpose(2, 0, 3, 1, 4).reshape(queries.shape)


def solution(mesh):
    in_specs = (
        P("outer", "inner", None, None),
        P("outer", "inner", None, None),
        P(),
        P(),
        P(),
        P("outer", "inner", None),
    )
    out_specs = P("outer", "inner", None, None)
    return jax.shard_map(
        on_device, mesh=mesh, in_specs=in_specs, out_specs=out_specs, check_vma=False
    )
```

```python
import jax
import jax.numpy as jnp
from jax import lax
from jax.experimental import pallas as pl
from jax.experimental.pallas import tpu as pltpu
from jax.sharding import PartitionSpec as P

SPAN = 8
HEAD = 128
HEADS = 8
ROWS = 8
GROUP = 64
FR = 6
CHUNK = SPAN * FR
KEYS = 128
MESSAGE = 3 * CHUNK + ROWS
PIECE = 16
SLABS = 4
NEG = -1e30
VMEM = pl.BlockSpec(memory_space=pltpu.VMEM)
SMEM = pl.BlockSpec(memory_space=pltpu.SMEM)


def swap_matrix(frames, rows, back):
    size = frames * rows
    a = lax.broadcasted_iota(jnp.int32, (size, size), 1 if back else 0)
    b = lax.broadcasted_iota(jnp.int32, (size, size), 0 if back else 1)
    hit = b == (a % frames) * rows + a // frames
    return jnp.where(hit, 1.0, 0.0).astype(jnp.bfloat16)


def block_number():
    return lax.axis_index("inner") * lax.axis_size("outer") + lax.axis_index("outer")


def prep_kernel(
    mask_hbm, x_hbm, w_hbm, q_hbm, out_hbm, mask_ref, x, w, q, total, out_ref, mask_sem, x_sem, w_sem, q_sem, out_sem
):
    depth = w.shape[0] // SLABS
    loads = []
    for slab in range(SLABS):
        span = slice(slab * depth, (slab + 1) * depth)
        loads.append(
            (
                pltpu.make_async_copy(w_hbm.at[span], w.at[span], w_sem.at[slab]),
                pltpu.make_async_copy(x_hbm.at[:, span], x.at[:, span], x_sem.at[slab]),
            )
        )
    q_load = pltpu.make_async_copy(q_hbm, q, q_sem)
    mask_load = pltpu.make_async_copy(mask_hbm, mask_ref, mask_sem)
    for load in loads[0] + loads[1]:
        load.start()
    mask_load.start()
    spatial = x.shape[0] // FR

    def place(part, pair, n):
        for half in range(2):
            cols = slice(half * HEAD, (half + 1) * HEAD)
            for group in range(spatial // ROWS):
                at = [f * spatial + group * ROWS for f in range(FR)]
                rows = jnp.concatenate([part[a : a + ROWS, cols] for a in at], axis=0)
                out_ref[group, 2 * pair + half, n * CHUNK : (n + 1) * CHUNK, :] = rows.astype(jnp.bfloat16)

    block = block_number()
    key = lax.broadcasted_iota(jnp.int32, (2 * ROWS, KEYS), 1) - (KEYS - CHUNK)
    reach = block % SPAN - (key + 96 * FR) // FR + 96
    seen = jnp.where(reach == 0, 1.0, 0.0)
    mask_load.wait()
    for m in range(1, SPAN + 1):
        visible = jnp.where((mask_ref[m] == 1) & (block >= m), 1.0, 0.0)
        seen = jnp.where(reach == m, visible, seen)
    seen = seen.astype(jnp.bfloat16)[0:ROWS]
    for group in range(spatial // ROWS):
        for head in range(HEADS):
            out_ref[group, head, 3 * CHUNK :, :] = seen

    for slab in range(SLABS):
        for load in loads[slab]:
            load.wait()
        if slab + 2 < SLABS:
            for load in loads[slab + 2]:
                load.start()
        if slab == 0:
            q_load.start()
        if slab == SLABS - 1:
            q_load.wait()
            for pair in range(HEADS // 2):
                place(q[:, pair * 2 * HEAD : (pair + 1) * 2 * HEAD].astype(jnp.float32), pair, 2)
        span = slice(slab * depth, (slab + 1) * depth)
        stores = []
        for pair in range(HEADS // 2):
            for n in range(2):
                first = (n * HEADS + 2 * pair) * HEAD
                cols = slice(first, first + 2 * HEAD)
                part = jnp.dot(x[:, span], w[span, cols], preferred_element_type=jnp.float32)
                if slab > 0:
                    part = part + total[:, cols]
                if slab < SLABS - 1:
                    total[:, cols] = part
                else:
                    place(part, pair, n)
            if slab == SLABS - 1:
                heads = slice(2 * pair, 2 * pair + 2)
                store = pltpu.make_async_copy(out_ref.at[:, heads], out_hbm.at[:, heads], out_sem.at[pair])
                store.start()
                stores.append(store)
    for store in stores:
        store.wait()


def prep(frames, queries, w_keyval, block_mask):
    tokens, width = frames.shape
    groups = tokens // FR // ROWS
    any_ = pl.BlockSpec(memory_space=pl.ANY)
    return pl.pallas_call(
        prep_kernel,
        in_specs=[any_] * 4,
        out_specs=any_,
        out_shape=jax.ShapeDtypeStruct((groups, HEADS, MESSAGE, HEAD), jnp.bfloat16),
        scratch_shapes=[
            pltpu.SMEM(block_mask.shape, block_mask.dtype),
            pltpu.VMEM(frames.shape, jnp.bfloat16),
            pltpu.VMEM(w_keyval.shape, jnp.bfloat16),
            pltpu.VMEM(queries.shape, jnp.bfloat16),
            pltpu.VMEM((tokens, w_keyval.shape[1]), jnp.float32),
            pltpu.VMEM((groups, HEADS, MESSAGE, HEAD), jnp.bfloat16),
            pltpu.SemaphoreType.DMA,
            pltpu.SemaphoreType.DMA((SLABS,)),
            pltpu.SemaphoreType.DMA((SLABS,)),
            pltpu.SemaphoreType.DMA,
            pltpu.SemaphoreType.DMA((HEADS // 2,)),
        ],
        compiler_params=pltpu.CompilerParams(vmem_limit_bytes=58 * 1024 * 1024),
        name="prep",
    )(block_mask, frames, w_keyval, queries)


def bias_of_head(bucket_ref, table_ref):
    head = block_number() % HEADS
    i = lax.broadcasted_iota(jnp.int32, (CHUNK, KEYS), 0)
    key = lax.broadcasted_iota(jnp.int32, (CHUNK, KEYS), 1) - (KEYS - CHUNK)
    off = i - key
    bias = jnp.full((CHUNK, KEYS), NEG, jnp.float32)
    for d in range(bucket_ref.shape[0]):
        bias = jnp.where(off == d, table_ref[head, bucket_ref[d]], bias)
    reach = i // FR - (key + 96 * FR) // FR + 96
    return jnp.where((reach >= 0) & (reach <= SPAN), bias, NEG)


def chunk_bias(base, rows):
    i = lax.broadcasted_iota(jnp.int32, (CHUNK, SPAN * ROWS), 0)
    b = lax.broadcasted_iota(jnp.int32, (CHUNK, SPAN * ROWS), 1)
    spread = jnp.where(i // FR * ROWS == b, 1.0, 0.0).astype(jnp.bfloat16)
    rows = rows.astype(jnp.float32).reshape(SPAN * ROWS, KEYS).astype(jnp.bfloat16)
    seen = jnp.dot(spread, rows, preferred_element_type=jnp.float32)
    return jnp.where(seen > 0.5, base, NEG)


def attend(held, start, bias):
    first = start + CHUNK - KEYS
    scores = [
        lax.dot_general(
            held[s, start : start + CHUNK, 2 * HEAD :],
            held[s, first : first + KEYS, 0:HEAD],
            (((1,), (1,)), ((), ())),
            preferred_element_type=jnp.float32,
        )
        for s in range(ROWS)
    ]
    scores = jnp.stack(scores, axis=0) * (HEAD**-0.5) + bias[None]
    expo = jnp.exp(scores - jnp.max(scores, axis=2, keepdims=True))
    weights = expo * (1.0 / jnp.sum(expo, axis=2, keepdims=True))
    weights = weights.astype(jnp.bfloat16)
    return [
        jnp.dot(
            weights[s], held[s, first : first + KEYS, HEAD : 2 * HEAD], preferred_element_type=jnp.float32
        ).astype(jnp.bfloat16)
        for s in range(ROWS)
    ]


def turn_in(held, swap, got_ref, blocks, parts, at):
    rows = [
        got_ref[blocks, n * CHUNK : (n + 1) * CHUNK, :].reshape(CHUNK * ROWS, HEAD) for n in range(parts)
    ]
    rows = jnp.concatenate(rows, axis=1)
    for piece in range(CHUNK // PIECE):
        part = rows[piece * PIECE * ROWS : (piece + 1) * PIECE * ROWS]
        turned = jnp.dot(swap, part, preferred_element_type=jnp.float32).astype(jnp.bfloat16)
        start = at + piece * PIECE
        held[:, start : start + PIECE, 0 : parts * HEAD] = turned.reshape(ROWS, PIECE, parts * HEAD)


def turn_out(out_ref, back, mixed, at):
    for piece in range(CHUNK // PIECE):
        rows = [m[piece * PIECE : (piece + 1) * PIECE] for m in mixed]
        rows = jnp.concatenate(rows, axis=0)
        start = at + piece * PIECE * ROWS
        out_ref[start : start + PIECE * ROWS, :] = jnp.dot(
            back, rows, preferred_element_type=jnp.float32
        ).astype(jnp.bfloat16)


def main_kernel(bucket_ref, table_ref, got_ref, out_ref, base_ref, held):
    base_ref[...] = bias_of_head(bucket_ref, table_ref)
    swap = swap_matrix(PIECE, ROWS, False)
    back = swap_matrix(PIECE, ROWS, True)
    lead = CHUNK
    held[:, 0:lead, :] = jnp.zeros((ROWS, lead, 3 * HEAD), jnp.bfloat16)
    for chunk in range(GROUP // SPAN):
        blocks = slice(chunk * SPAN, (chunk + 1) * SPAN)
        at = lead + chunk * CHUNK
        turn_in(held, swap, got_ref, blocks, 3, at)
        if chunk > 0:
            bias = chunk_bias(base_ref[...], got_ref[blocks, 3 * CHUNK :, :])
            turn_out(out_ref, back, attend(held, at, bias), chunk * CHUNK * ROWS)


def main_part(bucket_table, bias_table, got):
    frames = GROUP * FR
    return pl.pallas_call(
        main_kernel,
        in_specs=[SMEM, SMEM, VMEM],
        out_specs=[VMEM, VMEM],
        out_shape=[
            jax.ShapeDtypeStruct((frames * ROWS, HEAD), jnp.bfloat16),
            jax.ShapeDtypeStruct((CHUNK, KEYS), jnp.float32),
        ],
        scratch_shapes=[pltpu.VMEM((ROWS, CHUNK + frames, 3 * HEAD), jnp.bfloat16)],
        compiler_params=pltpu.CompilerParams(vmem_limit_bytes=40 * 1024 * 1024),
        cost_estimate=pl.CostEstimate(flops=2_000_000_000, bytes_accessed=16_000_000, transcendentals=0),
        name="main_part",
    )(bucket_table, bias_table, got)


def first_kernel(base_ref, got_ref, odd_ref, even_ref, rest_ref, out_ref, halo_ref, held):
    odd = (block_number() // GROUP) % 2 == 1

    @pl.when(odd)
    def _():
        halo_ref[...] = odd_ref[...]

    @pl.when(jnp.logical_not(odd))
    def _():
        halo_ref[...] = even_ref[...]

    swap = swap_matrix(PIECE, ROWS, False)
    back = swap_matrix(PIECE, ROWS, True)
    lead = KEYS - 2 * CHUNK
    blocks = slice(0, SPAN)
    held[:, 0:lead, :] = jnp.zeros((ROWS, lead, 3 * HEAD), jnp.bfloat16)
    turn_in(held, swap, halo_ref, blocks, 2, lead)
    turn_in(held, swap, got_ref, blocks, 3, lead + CHUNK)
    bias = chunk_bias(base_ref[...], got_ref[blocks, 3 * CHUNK :, :])
    turn_out(out_ref, back, attend(held, lead + CHUNK, bias), 0)


def first_part(base, got, odd, even, rest):
    return pl.pallas_call(
        first_kernel,
        in_specs=[VMEM] * 5,
        out_specs=VMEM,
        out_shape=jax.ShapeDtypeStruct(rest.shape, rest.dtype),
        scratch_shapes=[
            pltpu.VMEM(odd.shape, jnp.bfloat16),
            pltpu.VMEM((ROWS, KEYS, 3 * HEAD), jnp.bfloat16),
        ],
        input_output_aliases={4: 0},
        compiler_params=pltpu.CompilerParams(vmem_limit_bytes=40 * 1024 * 1024),
        name="first_part",
    )(base, got, odd, even, rest)


def exchange(array, groups):
    return lax.all_to_all(array, ("inner", "outer"), 0, 0, tiled=True, axis_index_groups=groups)


def on_device(frames, queries, w_keyval, bucket_table, bias_table, block_mask):
    n_outer = lax.axis_size("outer")
    n_blocks = lax.axis_size("inner") * n_outer
    groups = [list(range(g, g + GROUP)) for g in range(0, n_blocks, GROUP)]
    spatial, width = frames.shape[2:]

    sent = prep(
        frames.reshape(-1, width),
        queries.reshape(-1, queries.shape[3]),
        w_keyval,
        block_mask.reshape(-1),
    )
    got = exchange(sent.reshape(GROUP, MESSAGE, HEAD), groups)
    tail = got[GROUP - SPAN :, : 2 * CHUNK, :]
    halos = []
    for parity in range(2):
        partner = [2 * ((g + parity) // 2) + (g + parity + 1) % 2 - parity for g in range(len(groups))]
        partner = [p if 0 <= p < len(groups) else g for g, p in enumerate(partner)]
        perm = [(i, partner[i // GROUP] * GROUP + i % GROUP) for i in range(n_blocks)]
        halos.append(lax.ppermute(tail, ("inner", "outer"), perm))
    rest, base = main_part(bucket_table, bias_table.T, got)
    mixed = first_part(base, got, *halos, rest)
    out = exchange(mixed.reshape(GROUP, CHUNK, HEAD), groups)
    out = out.reshape(spatial // ROWS, HEADS, FR, ROWS, HEAD)
    return out.transpose(2, 0, 3, 1, 4).reshape(queries.shape)


def solution(mesh):
    in_specs = (
        P("outer", "inner", None, None),
        P("outer", "inner", None, None),
        P(),
        P(),
        P(),
        P("outer", "inner", None),
    )
    out_specs = P("outer", "inner", None, None)
    return jax.shard_map(
        on_device, mesh=mesh, in_specs=in_specs, out_specs=out_specs, check_vma=False
    )
```

```python
import jax
import jax.numpy as jnp
from jax import lax
from jax.experimental import pallas as pl
from jax.experimental.pallas import tpu as pltpu
from jax.sharding import PartitionSpec as P

SPAN = 8
HEAD = 128
HEADS = 8
ROWS = 8
GROUP = 64
FR = 6
CHUNK = SPAN * FR
KEYS = 128
MESSAGE = 3 * CHUNK + ROWS
PIECE = 16
SLABS = 4
NEG = -1e30
VMEM = pl.BlockSpec(memory_space=pltpu.VMEM)
SMEM = pl.BlockSpec(memory_space=pltpu.SMEM)


def swap_matrix(frames, rows, back):
    size = frames * rows
    a = lax.broadcasted_iota(jnp.int32, (size, size), 1 if back else 0)
    b = lax.broadcasted_iota(jnp.int32, (size, size), 0 if back else 1)
    hit = b == (a % frames) * rows + a // frames
    return jnp.where(hit, 1.0, 0.0).astype(jnp.bfloat16)


def block_number():
    return lax.axis_index("inner") * lax.axis_size("outer") + lax.axis_index("outer")


def prep_kernel(
    mask_hbm, x_hbm, w_hbm, q_hbm, out_hbm, mask_ref, x, w, q, total, out_ref, mask_sem, x_sem, w_sem, q_sem, out_sem
):
    depth = w.shape[0] // SLABS
    loads = []
    for slab in range(SLABS):
        span = slice(slab * depth, (slab + 1) * depth)
        loads.append(
            (
                pltpu.make_async_copy(w_hbm.at[span], w.at[span], w_sem.at[slab]),
                pltpu.make_async_copy(x_hbm.at[:, span], x.at[:, span], x_sem.at[slab]),
            )
        )
    q_load = pltpu.make_async_copy(q_hbm, q, q_sem)
    mask_load = pltpu.make_async_copy(mask_hbm, mask_ref, mask_sem)
    for load in loads[0] + loads[1]:
        load.start()
    mask_load.start()
    spatial = x.shape[0] // FR

    def place(part, pair, n):
        for half in range(2):
            cols = slice(half * HEAD, (half + 1) * HEAD)
            for group in range(spatial // ROWS):
                at = [f * spatial + group * ROWS for f in range(FR)]
                rows = jnp.concatenate([part[a : a + ROWS, cols] for a in at], axis=0)
                out_ref[group, 2 * pair + half, n * CHUNK : (n + 1) * CHUNK, :] = rows.astype(jnp.bfloat16)

    block = block_number()
    key = lax.broadcasted_iota(jnp.int32, (2 * ROWS, KEYS), 1) - (KEYS - CHUNK)
    reach = block % SPAN - (key + 96 * FR) // FR + 96
    seen = jnp.where(reach == 0, 1.0, 0.0)
    mask_load.wait()
    for m in range(1, SPAN + 1):
        visible = jnp.where((mask_ref[m] == 1) & (block >= m), 1.0, 0.0)
        seen = jnp.where(reach == m, visible, seen)
    seen = seen.astype(jnp.bfloat16)[0:ROWS]
    for group in range(spatial // ROWS):
        for head in range(HEADS):
            out_ref[group, head, 3 * CHUNK :, :] = seen

    for slab in range(SLABS):
        for load in loads[slab]:
            load.wait()
        if slab + 2 < SLABS:
            for load in loads[slab + 2]:
                load.start()
        if slab == 0:
            q_load.start()
        if slab == SLABS - 1:
            q_load.wait()
            for pair in range(HEADS // 2):
                place(q[:, pair * 2 * HEAD : (pair + 1) * 2 * HEAD].astype(jnp.float32), pair, 2)
        span = slice(slab * depth, (slab + 1) * depth)
        stores = []
        for pair in range(HEADS // 2):
            for n in range(2):
                first = (n * HEADS + 2 * pair) * HEAD
                cols = slice(first, first + 2 * HEAD)
                part = jnp.dot(x[:, span], w[span, cols], preferred_element_type=jnp.float32)
                if slab > 0:
                    part = part + total[:, cols]
                if slab < SLABS - 1:
                    total[:, cols] = part
                else:
                    place(part, pair, n)
            if slab == SLABS - 1:
                heads = slice(2 * pair, 2 * pair + 2)
                store = pltpu.make_async_copy(out_ref.at[:, heads], out_hbm.at[:, heads], out_sem.at[pair])
                store.start()
                stores.append(store)
    for store in stores:
        store.wait()


def prep(frames, queries, w_keyval, block_mask):
    tokens, width = frames.shape
    groups = tokens // FR // ROWS
    any_ = pl.BlockSpec(memory_space=pl.ANY)
    return pl.pallas_call(
        prep_kernel,
        in_specs=[any_] * 4,
        out_specs=any_,
        out_shape=jax.ShapeDtypeStruct((groups, HEADS, MESSAGE, HEAD), jnp.bfloat16),
        scratch_shapes=[
            pltpu.SMEM(block_mask.shape, block_mask.dtype),
            pltpu.VMEM(frames.shape, jnp.bfloat16),
            pltpu.VMEM(w_keyval.shape, jnp.bfloat16),
            pltpu.VMEM(queries.shape, jnp.bfloat16),
            pltpu.VMEM((tokens, w_keyval.shape[1]), jnp.float32),
            pltpu.VMEM((groups, HEADS, MESSAGE, HEAD), jnp.bfloat16),
            pltpu.SemaphoreType.DMA,
            pltpu.SemaphoreType.DMA((SLABS,)),
            pltpu.SemaphoreType.DMA((SLABS,)),
            pltpu.SemaphoreType.DMA,
            pltpu.SemaphoreType.DMA((HEADS // 2,)),
        ],
        compiler_params=pltpu.CompilerParams(vmem_limit_bytes=58 * 1024 * 1024),
        name="prep",
    )(block_mask, frames, w_keyval, queries)


def bias_of_head(bucket_ref, table_ref):
    head = block_number() % HEADS
    i = lax.broadcasted_iota(jnp.int32, (CHUNK, KEYS), 0)
    key = lax.broadcasted_iota(jnp.int32, (CHUNK, KEYS), 1) - (KEYS - CHUNK)
    off = i - key
    bias = jnp.full((CHUNK, KEYS), NEG, jnp.float32)
    for d in range(bucket_ref.shape[0]):
        bias = jnp.where(off == d, table_ref[head, bucket_ref[d]], bias)
    reach = i // FR - (key + 96 * FR) // FR + 96
    return jnp.where((reach >= 0) & (reach <= SPAN), bias, NEG)


def chunk_bias(base, rows):
    i = lax.broadcasted_iota(jnp.int32, (CHUNK, SPAN * ROWS), 0)
    b = lax.broadcasted_iota(jnp.int32, (CHUNK, SPAN * ROWS), 1)
    spread = jnp.where(i // FR * ROWS == b, 1.0, 0.0).astype(jnp.bfloat16)
    rows = rows.astype(jnp.float32).reshape(SPAN * ROWS, KEYS).astype(jnp.bfloat16)
    seen = jnp.dot(spread, rows, preferred_element_type=jnp.float32)
    return jnp.where(seen > 0.5, base, NEG)


def attend(held, start, bias):
    first = start + CHUNK - KEYS
    scores = [
        lax.dot_general(
            held[s, start : start + CHUNK, 2 * HEAD :],
            held[s, first : first + KEYS, 0:HEAD],
            (((1,), (1,)), ((), ())),
            preferred_element_type=jnp.float32,
        )
        for s in range(ROWS)
    ]
    scores = jnp.stack(scores, axis=0) * (HEAD**-0.5) + bias[None]
    expo = jnp.exp(scores - jnp.max(scores, axis=2, keepdims=True))
    weights = expo * (1.0 / jnp.sum(expo, axis=2, keepdims=True))
    weights = weights.astype(jnp.bfloat16)
    return [
        jnp.dot(
            weights[s], held[s, first : first + KEYS, HEAD : 2 * HEAD], preferred_element_type=jnp.float32
        ).astype(jnp.bfloat16)
        for s in range(ROWS)
    ]


def turn_in(held, swap, got_ref, blocks, parts, at):
    rows = [
        got_ref[blocks, n * CHUNK : (n + 1) * CHUNK, :].reshape(CHUNK * ROWS, HEAD) for n in range(parts)
    ]
    rows = jnp.concatenate(rows, axis=1)
    for piece in range(CHUNK // PIECE):
        part = rows[piece * PIECE * ROWS : (piece + 1) * PIECE * ROWS]
        turned = jnp.dot(swap, part, preferred_element_type=jnp.float32).astype(jnp.bfloat16)
        start = at + piece * PIECE
        held[:, start : start + PIECE, 0 : parts * HEAD] = turned.reshape(ROWS, PIECE, parts * HEAD)


def turn_out(out_ref, back, mixed, at):
    for piece in range(CHUNK // PIECE):
        rows = [m[piece * PIECE : (piece + 1) * PIECE] for m in mixed]
        rows = jnp.concatenate(rows, axis=0)
        start = at + piece * PIECE * ROWS
        out_ref[start : start + PIECE * ROWS, :] = jnp.dot(
            back, rows, preferred_element_type=jnp.float32
        ).astype(jnp.bfloat16)


def main_kernel(bucket_ref, table_ref, got_ref, out_ref, bias_ref, first_ref, held):
    base = bias_of_head(bucket_ref, table_ref)
    swap = swap_matrix(PIECE, ROWS, False)
    back = swap_matrix(PIECE, ROWS, True)
    lead = CHUNK
    held[:, 0:lead, :] = jnp.zeros((ROWS, lead, 3 * HEAD), jnp.bfloat16)
    for chunk in range(GROUP // SPAN):
        blocks = slice(chunk * SPAN, (chunk + 1) * SPAN)
        at = lead + chunk * CHUNK
        turn_in(held, swap, got_ref, blocks, 3, at)
        bias = chunk_bias(base, got_ref[blocks, 3 * CHUNK :, :])
        if chunk > 0:
            turn_out(out_ref, back, attend(held, at, bias), chunk * CHUNK * ROWS)
        else:
            bias_ref[...] = bias
            first_ref[:, : KEYS - CHUNK, :] = jnp.zeros((ROWS, KEYS - CHUNK, 3 * HEAD), jnp.bfloat16)
            first_ref[:, KEYS - CHUNK :, :] = held[:, at : at + CHUNK, :]


def main_part(bucket_table, bias_table, got):
    frames = GROUP * FR
    return pl.pallas_call(
        main_kernel,
        in_specs=[SMEM, SMEM, VMEM],
        out_specs=[VMEM] * 3,
        out_shape=[
            jax.ShapeDtypeStruct((frames * ROWS, HEAD), jnp.bfloat16),
            jax.ShapeDtypeStruct((CHUNK, KEYS), jnp.float32),
            jax.ShapeDtypeStruct((ROWS, KEYS, 3 * HEAD), jnp.bfloat16),
        ],
        scratch_shapes=[pltpu.VMEM((ROWS, CHUNK + frames, 3 * HEAD), jnp.bfloat16)],
        compiler_params=pltpu.CompilerParams(vmem_limit_bytes=40 * 1024 * 1024),
        cost_estimate=pl.CostEstimate(flops=2_000_000_000, bytes_accessed=16_000_000, transcendentals=0),
        name="main_part",
    )(bucket_table, bias_table, got)


def first_kernel(bias_ref, halo_ref, own_ref, rest_ref, out_ref, held):
    swap = swap_matrix(PIECE, ROWS, False)
    back = swap_matrix(PIECE, ROWS, True)
    turn_in(held, swap, halo_ref, slice(0, SPAN), 2, KEYS - 2 * CHUNK)
    turn_out(out_ref, back, attend(held, KEYS - CHUNK, bias_ref[...]), 0)


def first_part(bias, halo, own, rest):
    return pl.pallas_call(
        first_kernel,
        in_specs=[VMEM] * 4,
        out_specs=[VMEM] * 2,
        out_shape=[jax.ShapeDtypeStruct(a.shape, a.dtype) for a in (rest, own)],
        input_output_aliases={2: 1, 3: 0},
        compiler_params=pltpu.CompilerParams(vmem_limit_bytes=40 * 1024 * 1024),
        name="first_part",
    )(bias, halo, own, rest)[0]


def exchange(array, groups):
    return lax.all_to_all(array, ("inner", "outer"), 0, 0, tiled=True, axis_index_groups=groups)


def on_device(frames, queries, w_keyval, bucket_table, bias_table, block_mask):
    n_outer = lax.axis_size("outer")
    n_blocks = lax.axis_size("inner") * n_outer
    groups = [list(range(g, g + GROUP)) for g in range(0, n_blocks, GROUP)]
    spatial, width = frames.shape[2:]

    sent = prep(
        frames.reshape(-1, width),
        queries.reshape(-1, queries.shape[3]),
        w_keyval,
        block_mask.reshape(-1),
    )
    got = exchange(sent.reshape(GROUP, MESSAGE, HEAD), groups)
    perm = [(i, i + GROUP) for i in range(n_blocks - GROUP)]
    halo = lax.ppermute(got[GROUP - SPAN :, : 2 * CHUNK, :], ("inner", "outer"), perm)
    rest, bias, own = main_part(bucket_table, bias_table.T, got)
    mixed = first_part(bias, halo, own, rest)
    out = exchange(mixed.reshape(GROUP, CHUNK, HEAD), groups)
    out = out.reshape(spatial // ROWS, HEADS, FR, ROWS, HEAD)
    return out.transpose(2, 0, 3, 1, 4).reshape(queries.shape)


def solution(mesh):
    in_specs = (
        P("outer", "inner", None, None),
        P("outer", "inner", None, None),
        P(),
        P(),
        P(),
        P("outer", "inner", None),
    )
    out_specs = P("outer", "inner", None, None)
    return jax.shard_map(
        on_device, mesh=mesh, in_specs=in_specs, out_specs=out_specs, check_vma=False
    )
```

```python
import jax
import jax.numpy as jnp
from jax import lax
from jax.experimental import pallas as pl
from jax.experimental.pallas import tpu as pltpu
from jax.sharding import PartitionSpec as P

SPAN = 8
HEAD = 128
HEADS = 8
ROWS = 8
GROUP = 64
FR = 6
CHUNK = SPAN * FR
KEYS = 128
MESSAGE = 3 * CHUNK + ROWS
PIECE = 16
SLABS = 4
NEG = -1e30
VMEM = pl.BlockSpec(memory_space=pltpu.VMEM)
SMEM = pl.BlockSpec(memory_space=pltpu.SMEM)


def swap_matrix(frames, rows, back):
    size = frames * rows
    a = lax.broadcasted_iota(jnp.int32, (size, size), 1 if back else 0)
    b = lax.broadcasted_iota(jnp.int32, (size, size), 0 if back else 1)
    hit = b == (a % frames) * rows + a // frames
    return jnp.where(hit, 1.0, 0.0).astype(jnp.bfloat16)


def block_number():
    return lax.axis_index("inner") * lax.axis_size("outer") + lax.axis_index("outer")


def prep_kernel(
    mask_hbm, x_hbm, w_hbm, q_hbm, out_hbm, mask_ref, x, w, q, total, out_ref, mask_sem, x_sem, w_sem, q_sem, out_sem
):
    depth = w.shape[0] // SLABS
    loads = []
    for slab in range(SLABS):
        span = slice(slab * depth, (slab + 1) * depth)
        loads.append(
            (
                pltpu.make_async_copy(w_hbm.at[span], w.at[span], w_sem.at[slab]),
                pltpu.make_async_copy(x_hbm.at[:, span], x.at[:, span], x_sem.at[slab]),
            )
        )
    q_load = pltpu.make_async_copy(q_hbm, q, q_sem)
    mask_load = pltpu.make_async_copy(mask_hbm, mask_ref, mask_sem)
    for load in loads[0] + loads[1]:
        load.start()
    mask_load.start()
    spatial = x.shape[0] // FR

    def place(part, pair, n):
        for half in range(2):
            cols = slice(half * HEAD, (half + 1) * HEAD)
            for group in range(spatial // ROWS):
                at = [f * spatial + group * ROWS for f in range(FR)]
                rows = jnp.concatenate([part[a : a + ROWS, cols] for a in at], axis=0)
                out_ref[group, 2 * pair + half, n * CHUNK : (n + 1) * CHUNK, :] = rows.astype(jnp.bfloat16)

    block = block_number()
    key = lax.broadcasted_iota(jnp.int32, (2 * ROWS, KEYS), 1) - (KEYS - CHUNK)
    reach = block % SPAN - (key + 96 * FR) // FR + 96
    seen = jnp.where(reach == 0, 1.0, 0.0)
    mask_load.wait()
    for m in range(1, SPAN + 1):
        visible = jnp.where((mask_ref[m] == 1) & (block >= m), 1.0, 0.0)
        seen = jnp.where(reach == m, visible, seen)
    seen = seen.astype(jnp.bfloat16)[0:ROWS]
    for group in range(spatial // ROWS):
        for head in range(HEADS):
            out_ref[group, head, 3 * CHUNK :, :] = seen

    for slab in range(SLABS):
        for load in loads[slab]:
            load.wait()
        if slab + 2 < SLABS:
            for load in loads[slab + 2]:
                load.start()
        if slab == 0:
            q_load.start()
        if slab == SLABS - 1:
            q_load.wait()
            for pair in range(HEADS // 2):
                place(q[:, pair * 2 * HEAD : (pair + 1) * 2 * HEAD].astype(jnp.float32), pair, 2)
        span = slice(slab * depth, (slab + 1) * depth)
        stores = []
        for pair in range(HEADS // 2):
            for n in range(2):
                first = (n * HEADS + 2 * pair) * HEAD
                cols = slice(first, first + 2 * HEAD)
                part = jnp.dot(x[:, span], w[span, cols], preferred_element_type=jnp.float32)
                if slab > 0:
                    part = part + total[:, cols]
                if slab < SLABS - 1:
                    total[:, cols] = part
                else:
                    place(part, pair, n)
            if slab == SLABS - 1:
                heads = slice(2 * pair, 2 * pair + 2)
                store = pltpu.make_async_copy(out_ref.at[:, heads], out_hbm.at[:, heads], out_sem.at[pair])
                store.start()
                stores.append(store)
    for store in stores:
        store.wait()


def prep(frames, queries, w_keyval, block_mask):
    tokens, width = frames.shape
    groups = tokens // FR // ROWS
    any_ = pl.BlockSpec(memory_space=pl.ANY)
    return pl.pallas_call(
        prep_kernel,
        in_specs=[any_] * 4,
        out_specs=any_,
        out_shape=jax.ShapeDtypeStruct((groups, HEADS, MESSAGE, HEAD), jnp.bfloat16),
        scratch_shapes=[
            pltpu.SMEM(block_mask.shape, block_mask.dtype),
            pltpu.VMEM(frames.shape, jnp.bfloat16),
            pltpu.VMEM(w_keyval.shape, jnp.bfloat16),
            pltpu.VMEM(queries.shape, jnp.bfloat16),
            pltpu.VMEM((tokens, w_keyval.shape[1]), jnp.float32),
            pltpu.VMEM((groups, HEADS, MESSAGE, HEAD), jnp.bfloat16),
            pltpu.SemaphoreType.DMA,
            pltpu.SemaphoreType.DMA((SLABS,)),
            pltpu.SemaphoreType.DMA((SLABS,)),
            pltpu.SemaphoreType.DMA,
            pltpu.SemaphoreType.DMA((HEADS // 2,)),
        ],
        compiler_params=pltpu.CompilerParams(vmem_limit_bytes=58 * 1024 * 1024),
        name="prep",
    )(block_mask, frames, w_keyval, queries)


def bias_of_head(bucket_ref, table_ref):
    head = block_number() % HEADS
    i = lax.broadcasted_iota(jnp.int32, (CHUNK, KEYS), 0)
    key = lax.broadcasted_iota(jnp.int32, (CHUNK, KEYS), 1) - (KEYS - CHUNK)
    off = i - key
    bias = jnp.full((CHUNK, KEYS), NEG, jnp.float32)
    for d in range(bucket_ref.shape[0]):
        bias = jnp.where(off == d, table_ref[head, bucket_ref[d]], bias)
    reach = i // FR - (key + 96 * FR) // FR + 96
    return jnp.where((reach >= 0) & (reach <= SPAN), bias, NEG)


def chunk_bias(base, rows):
    i = lax.broadcasted_iota(jnp.int32, (CHUNK, SPAN * ROWS), 0)
    b = lax.broadcasted_iota(jnp.int32, (CHUNK, SPAN * ROWS), 1)
    spread = jnp.where(i // FR * ROWS == b, 1.0, 0.0).astype(jnp.bfloat16)
    rows = rows.astype(jnp.float32).reshape(SPAN * ROWS, KEYS).astype(jnp.bfloat16)
    seen = jnp.dot(spread, rows, preferred_element_type=jnp.float32)
    return jnp.where(seen > 0.5, base, NEG)


def score(held, start, bias):
    first = start + CHUNK - KEYS
    scores = []
    for s in range(0, ROWS, 2):
        q = jnp.concatenate([held[t, start : start + CHUNK, 2 * HEAD :] for t in (s, s + 1)], axis=0)
        k = jnp.concatenate([held[t, first : first + KEYS, 0:HEAD] for t in (s, s + 1)], axis=0)
        both = lax.dot_general(q, k, (((1,), (1,)), ((), ())), preferred_element_type=jnp.float32)
        scores += [both[0:CHUNK, 0:KEYS], both[CHUNK:, KEYS:]]
    return jnp.stack(scores, axis=0) * (HEAD**-0.5) + bias[None]


def mix(held, start, scores):
    first = start + CHUNK - KEYS
    expo = jnp.exp(scores - jnp.max(scores, axis=2, keepdims=True))
    weights = expo * (1.0 / jnp.sum(expo, axis=2, keepdims=True))
    weights = weights.astype(jnp.bfloat16)
    mixed = []
    for s in range(0, ROWS, 2):
        v = jnp.concatenate([held[t, first : first + KEYS, HEAD : 2 * HEAD] for t in (s, s + 1)], axis=1)
        both = jnp.dot(weights[s : s + 2].reshape(2 * CHUNK, KEYS), v, preferred_element_type=jnp.float32)
        both = both.astype(jnp.bfloat16)
        mixed += [both[0:CHUNK, 0:HEAD], both[CHUNK:, HEAD:]]
    return mixed


def attend(held, start, bias):
    return mix(held, start, score(held, start, bias))


def turn_in(held, swap, got_ref, blocks, parts, at):
    rows = [
        got_ref[blocks, n * CHUNK : (n + 1) * CHUNK, :].reshape(CHUNK * ROWS, HEAD) for n in range(parts)
    ]
    rows = jnp.concatenate(rows, axis=1)
    for piece in range(CHUNK // PIECE):
        part = rows[piece * PIECE * ROWS : (piece + 1) * PIECE * ROWS]
        turned = jnp.dot(swap, part, preferred_element_type=jnp.float32).astype(jnp.bfloat16)
        start = at + piece * PIECE
        held[:, start : start + PIECE, 0 : parts * HEAD] = turned.reshape(ROWS, PIECE, parts * HEAD)


def turn_out(out_ref, back, mixed, at):
    for piece in range(CHUNK // PIECE):
        rows = [m[piece * PIECE : (piece + 1) * PIECE] for m in mixed]
        rows = jnp.concatenate(rows, axis=0)
        start = at + piece * PIECE * ROWS
        out_ref[start : start + PIECE * ROWS, :] = jnp.dot(
            back, rows, preferred_element_type=jnp.float32
        ).astype(jnp.bfloat16)


def main_kernel(bucket_ref, table_ref, got_ref, out_ref, bias_ref, first_ref, held):
    base = bias_of_head(bucket_ref, table_ref)
    swap = swap_matrix(PIECE, ROWS, False)
    back = swap_matrix(PIECE, ROWS, True)
    lead = CHUNK
    held[:, 0:lead, :] = jnp.zeros((ROWS, lead, 3 * HEAD), jnp.bfloat16)
    for chunk in range(GROUP // SPAN):
        turn_in(held, swap, got_ref, slice(chunk * SPAN, (chunk + 1) * SPAN), 3, lead + chunk * CHUNK)

    def bias_of(chunk):
        return chunk_bias(base, got_ref[chunk * SPAN : (chunk + 1) * SPAN, 3 * CHUNK :, :])

    bias_ref[...] = bias_of(0)
    first_ref[:, : KEYS - CHUNK, :] = jnp.zeros((ROWS, KEYS - CHUNK, 3 * HEAD), jnp.bfloat16)
    first_ref[:, KEYS - CHUNK :, :] = held[:, lead : lead + CHUNK, :]
    chunks = GROUP // SPAN
    scores = score(held, lead + CHUNK, bias_of(1))
    mixed = None
    for chunk in range(1, chunks):
        after = None
        if chunk + 1 < chunks:
            after = score(held, lead + (chunk + 1) * CHUNK, bias_of(chunk + 1))
        if mixed is not None:
            turn_out(out_ref, back, mixed, (chunk - 1) * CHUNK * ROWS)
        mixed = mix(held, lead + chunk * CHUNK, scores)
        scores = after
    turn_out(out_ref, back, mixed, (chunks - 1) * CHUNK * ROWS)


def main_part(bucket_table, bias_table, got):
    frames = GROUP * FR
    return pl.pallas_call(
        main_kernel,
        in_specs=[SMEM, SMEM, VMEM],
        out_specs=[VMEM] * 3,
        out_shape=[
            jax.ShapeDtypeStruct((frames * ROWS, HEAD), jnp.bfloat16),
            jax.ShapeDtypeStruct((CHUNK, KEYS), jnp.float32),
            jax.ShapeDtypeStruct((ROWS, KEYS, 3 * HEAD), jnp.bfloat16),
        ],
        scratch_shapes=[pltpu.VMEM((ROWS, CHUNK + frames, 3 * HEAD), jnp.bfloat16)],
        compiler_params=pltpu.CompilerParams(vmem_limit_bytes=40 * 1024 * 1024),
        cost_estimate=pl.CostEstimate(flops=2_000_000_000, bytes_accessed=16_000_000, transcendentals=0),
        name="main_part",
    )(bucket_table, bias_table, got)


def first_kernel(bias_ref, halo_ref, own_ref, rest_ref, out_ref, held):
    swap = swap_matrix(PIECE, ROWS, False)
    back = swap_matrix(PIECE, ROWS, True)
    turn_in(held, swap, halo_ref, slice(0, SPAN), 2, KEYS - 2 * CHUNK)
    turn_out(out_ref, back, attend(held, KEYS - CHUNK, bias_ref[...]), 0)


def first_part(bias, halo, own, rest):
    return pl.pallas_call(
        first_kernel,
        in_specs=[VMEM] * 4,
        out_specs=[VMEM] * 2,
        out_shape=[jax.ShapeDtypeStruct(a.shape, a.dtype) for a in (rest, own)],
        input_output_aliases={2: 1, 3: 0},
        compiler_params=pltpu.CompilerParams(vmem_limit_bytes=40 * 1024 * 1024),
        name="first_part",
    )(bias, halo, own, rest)[0]


def exchange(array, groups):
    return lax.all_to_all(array, ("inner", "outer"), 0, 0, tiled=True, axis_index_groups=groups)


def on_device(frames, queries, w_keyval, bucket_table, bias_table, block_mask):
    n_outer = lax.axis_size("outer")
    n_blocks = lax.axis_size("inner") * n_outer
    groups = [list(range(g, g + GROUP)) for g in range(0, n_blocks, GROUP)]
    spatial, width = frames.shape[2:]

    sent = prep(
        frames.reshape(-1, width),
        queries.reshape(-1, queries.shape[3]),
        w_keyval,
        block_mask.reshape(-1),
    )
    got = exchange(sent.reshape(GROUP, MESSAGE, HEAD), groups)
    perm = [(i, i + GROUP) for i in range(n_blocks - GROUP)]
    halo = lax.ppermute(got[GROUP - SPAN :, : 2 * CHUNK, :], ("inner", "outer"), perm)
    rest, bias, own = main_part(bucket_table, bias_table.T, got)
    mixed = first_part(bias, halo, own, rest)
    out = exchange(mixed.reshape(GROUP, CHUNK, HEAD), groups)
    out = out.reshape(spatial // ROWS, HEADS, FR, ROWS, HEAD)
    return out.transpose(2, 0, 3, 1, 4).reshape(queries.shape)


def solution(mesh):
    in_specs = (
        P("outer", "inner", None, None),
        P("outer", "inner", None, None),
        P(),
        P(),
        P(),
        P("outer", "inner", None),
    )
    out_specs = P("outer", "inner", None, None)
    return jax.shard_map(
        on_device, mesh=mesh, in_specs=in_specs, out_specs=out_specs, check_vma=False
    )
```

```python
import jax
import jax.numpy as jnp
from jax import lax
from jax.experimental import pallas as pl
from jax.experimental.pallas import tpu as pltpu
from jax.sharding import PartitionSpec as P

SPAN = 8
HEAD = 128
HEADS = 8
ROWS = 8
GROUP = 64
FR = 6
CHUNK = SPAN * FR
KEYS = 128
MESSAGE = 3 * CHUNK + ROWS
PIECE = 16
SLABS = 4
NEG = -1e30
VMEM = pl.BlockSpec(memory_space=pltpu.VMEM)
SMEM = pl.BlockSpec(memory_space=pltpu.SMEM)


def swap_matrix(frames, rows, back):
    size = frames * rows
    a = lax.broadcasted_iota(jnp.int32, (size, size), 1 if back else 0)
    b = lax.broadcasted_iota(jnp.int32, (size, size), 0 if back else 1)
    hit = b == (a % frames) * rows + a // frames
    return jnp.where(hit, 1.0, 0.0).astype(jnp.bfloat16)


def block_number():
    return lax.axis_index("inner") * lax.axis_size("outer") + lax.axis_index("outer")


def prep_kernel(
    mask_hbm, x_hbm, w_hbm, q_hbm, out_hbm, mask_ref, x, w, q, total, out_ref, mask_sem, x_sem, w_sem, q_sem, out_sem
):
    depth = w.shape[0] // SLABS
    loads = []
    for slab in range(SLABS):
        span = slice(slab * depth, (slab + 1) * depth)
        loads.append(
            (
                pltpu.make_async_copy(w_hbm.at[span], w.at[span], w_sem.at[slab]),
                pltpu.make_async_copy(x_hbm.at[:, span], x.at[:, span], x_sem.at[slab]),
            )
        )
    q_load = pltpu.make_async_copy(q_hbm, q, q_sem)
    mask_load = pltpu.make_async_copy(mask_hbm, mask_ref, mask_sem)
    for load in loads[0] + loads[1]:
        load.start()
    mask_load.start()
    spatial = x.shape[0] // FR

    def place(part, pair, n):
        for half in range(2):
            cols = slice(half * HEAD, (half + 1) * HEAD)
            for group in range(spatial // ROWS):
                at = [f * spatial + group * ROWS for f in range(FR)]
                rows = jnp.concatenate([part[a : a + ROWS, cols] for a in at], axis=0)
                out_ref[group, 2 * pair + half, n * CHUNK : (n + 1) * CHUNK, :] = rows.astype(jnp.bfloat16)

    block = block_number()
    key = lax.broadcasted_iota(jnp.int32, (2 * ROWS, KEYS), 1) - (KEYS - CHUNK)
    reach = block % SPAN - (key + 96 * FR) // FR + 96
    seen = jnp.where(reach == 0, 1.0, 0.0)
    mask_load.wait()
    for m in range(1, SPAN + 1):
        visible = jnp.where((mask_ref[m] == 1) & (block >= m), 1.0, 0.0)
        seen = jnp.where(reach == m, visible, seen)
    seen = seen.astype(jnp.bfloat16)[0:ROWS]
    for group in range(spatial // ROWS):
        for head in range(HEADS):
            out_ref[group, head, 3 * CHUNK :, :] = seen

    for slab in range(SLABS):
        for load in loads[slab]:
            load.wait()
        if slab + 2 < SLABS:
            for load in loads[slab + 2]:
                load.start()
        if slab == 0:
            q_load.start()
        if slab == SLABS - 1:
            q_load.wait()
            for pair in range(HEADS // 2):
                place(q[:, pair * 2 * HEAD : (pair + 1) * 2 * HEAD].astype(jnp.float32), pair, 2)
        span = slice(slab * depth, (slab + 1) * depth)
        stores = []
        for pair in range(HEADS // 2):
            for n in range(2):
                first = (n * HEADS + 2 * pair) * HEAD
                cols = slice(first, first + 2 * HEAD)
                part = jnp.dot(x[:, span], w[span, cols], preferred_element_type=jnp.float32)
                if slab > 0:
                    part = part + total[:, cols]
                if slab < SLABS - 1:
                    total[:, cols] = part
                else:
                    place(part, pair, n)
            if slab == SLABS - 1:
                heads = slice(2 * pair, 2 * pair + 2)
                store = pltpu.make_async_copy(out_ref.at[:, heads], out_hbm.at[:, heads], out_sem.at[pair])
                store.start()
                stores.append(store)
    for store in stores:
        store.wait()


def prep(frames, queries, w_keyval, block_mask):
    tokens, width = frames.shape
    groups = tokens // FR // ROWS
    any_ = pl.BlockSpec(memory_space=pl.ANY)
    return pl.pallas_call(
        prep_kernel,
        in_specs=[any_] * 4,
        out_specs=any_,
        out_shape=jax.ShapeDtypeStruct((groups, HEADS, MESSAGE, HEAD), jnp.bfloat16),
        scratch_shapes=[
            pltpu.SMEM(block_mask.shape, block_mask.dtype),
            pltpu.VMEM(frames.shape, jnp.bfloat16),
            pltpu.VMEM(w_keyval.shape, jnp.bfloat16),
            pltpu.VMEM(queries.shape, jnp.bfloat16),
            pltpu.VMEM((tokens, w_keyval.shape[1]), jnp.float32),
            pltpu.VMEM((groups, HEADS, MESSAGE, HEAD), jnp.bfloat16),
            pltpu.SemaphoreType.DMA,
            pltpu.SemaphoreType.DMA((SLABS,)),
            pltpu.SemaphoreType.DMA((SLABS,)),
            pltpu.SemaphoreType.DMA,
            pltpu.SemaphoreType.DMA((HEADS // 2,)),
        ],
        compiler_params=pltpu.CompilerParams(vmem_limit_bytes=58 * 1024 * 1024),
        name="prep",
    )(block_mask, frames, w_keyval, queries)


def bias_of_head(bucket_ref, table_ref):
    head = block_number() % HEADS
    i = lax.broadcasted_iota(jnp.int32, (CHUNK, KEYS), 0)
    key = lax.broadcasted_iota(jnp.int32, (CHUNK, KEYS), 1) - (KEYS - CHUNK)
    off = i - key
    bias = jnp.full((CHUNK, KEYS), NEG, jnp.float32)
    for d in range(bucket_ref.shape[0]):
        bias = jnp.where(off == d, table_ref[head, bucket_ref[d]], bias)
    reach = i // FR - (key + 96 * FR) // FR + 96
    return jnp.where((reach >= 0) & (reach <= SPAN), bias, NEG)


def chunk_bias(base, rows):
    i = lax.broadcasted_iota(jnp.int32, (CHUNK, SPAN * ROWS), 0)
    b = lax.broadcasted_iota(jnp.int32, (CHUNK, SPAN * ROWS), 1)
    spread = jnp.where(i // FR * ROWS == b, 1.0, 0.0).astype(jnp.bfloat16)
    rows = rows.astype(jnp.float32).reshape(SPAN * ROWS, KEYS).astype(jnp.bfloat16)
    seen = jnp.dot(spread, rows, preferred_element_type=jnp.float32)
    return jnp.where(seen > 0.5, base, NEG)


def score(held, start, bias):
    first = start + CHUNK - KEYS
    scores = []
    for s in range(0, ROWS, 2):
        q = jnp.concatenate([held[t, start : start + CHUNK, 2 * HEAD :] for t in (s, s + 1)], axis=0)
        k = jnp.concatenate([held[t, first : first + KEYS, 0:HEAD] for t in (s, s + 1)], axis=0)
        both = lax.dot_general(q, k, (((1,), (1,)), ((), ())), preferred_element_type=jnp.float32)
        scores += [both[0:CHUNK, 0:KEYS], both[CHUNK:, KEYS:]]
    return jnp.stack(scores, axis=0) * (HEAD**-0.5) + bias[None]


def mix(held, start, scores):
    first = start + CHUNK - KEYS
    expo = jnp.exp(scores - jnp.max(scores, axis=2, keepdims=True))
    weights = expo * (1.0 / jnp.sum(expo, axis=2, keepdims=True))
    weights = weights.astype(jnp.bfloat16)
    mixed = []
    for s in range(0, ROWS, 2):
        v = jnp.concatenate([held[t, first : first + KEYS, HEAD : 2 * HEAD] for t in (s, s + 1)], axis=1)
        both = jnp.dot(weights[s : s + 2].reshape(2 * CHUNK, KEYS), v, preferred_element_type=jnp.float32)
        both = both.astype(jnp.bfloat16)
        mixed += [both[0:CHUNK, 0:HEAD], both[CHUNK:, HEAD:]]
    return mixed


def attend(held, start, bias):
    return mix(held, start, score(held, start, bias))


def turn_in(held, swap, got_ref, blocks, parts, at):
    rows = [
        got_ref[blocks, n * CHUNK : (n + 1) * CHUNK, :].reshape(CHUNK * ROWS, HEAD) for n in range(parts)
    ]
    rows = jnp.concatenate(rows, axis=1)
    for piece in range(CHUNK // PIECE):
        part = rows[piece * PIECE * ROWS : (piece + 1) * PIECE * ROWS]
        turned = jnp.dot(swap, part, preferred_element_type=jnp.float32).astype(jnp.bfloat16)
        start = at + piece * PIECE
        held[:, start : start + PIECE, 0 : parts * HEAD] = turned.reshape(ROWS, PIECE, parts * HEAD)


def turn_out(out_ref, back, mixed, at):
    for piece in range(CHUNK // PIECE):
        rows = [m[piece * PIECE : (piece + 1) * PIECE] for m in mixed]
        rows = jnp.concatenate(rows, axis=0)
        start = at + piece * PIECE * ROWS
        out_ref[start : start + PIECE * ROWS, :] = jnp.dot(
            back, rows, preferred_element_type=jnp.float32
        ).astype(jnp.bfloat16)


def main_kernel(bucket_ref, table_ref, got_ref, out_ref, bias_ref, first_ref, held):
    base = bias_of_head(bucket_ref, table_ref)
    swap = swap_matrix(PIECE, ROWS, False)
    back = swap_matrix(PIECE, ROWS, True)
    lead = CHUNK
    held[:, 0:lead, :] = jnp.zeros((ROWS, lead, 3 * HEAD), jnp.bfloat16)
    for chunk in range(GROUP // SPAN):
        turn_in(held, swap, got_ref, slice(chunk * SPAN, (chunk + 1) * SPAN), 3, lead + chunk * CHUNK)

    def bias_of(chunk):
        return chunk_bias(base, got_ref[chunk * SPAN : (chunk + 1) * SPAN, 3 * CHUNK :, :])

    bias_ref[...] = bias_of(0)
    first_ref[:, : KEYS - CHUNK, :] = jnp.zeros((ROWS, KEYS - CHUNK, 3 * HEAD), jnp.bfloat16)
    first_ref[:, KEYS - CHUNK :, :] = held[:, lead : lead + CHUNK, :]
    chunks = GROUP // SPAN
    scores = score(held, lead + CHUNK, bias_of(1))
    mixed = None
    for chunk in range(1, chunks):
        after = None
        if chunk + 1 < chunks:
            after = score(held, lead + (chunk + 1) * CHUNK, bias_of(chunk + 1))
        if mixed is not None:
            turn_out(out_ref, back, mixed, (chunk - 1) * CHUNK * ROWS)
        mixed = mix(held, lead + chunk * CHUNK, scores)
        scores = after
    turn_out(out_ref, back, mixed, (chunks - 1) * CHUNK * ROWS)


def main_part(bucket_table, bias_table, got):
    frames = GROUP * FR
    return pl.pallas_call(
        main_kernel,
        in_specs=[SMEM, SMEM, VMEM],
        out_specs=[VMEM] * 3,
        out_shape=[
            jax.ShapeDtypeStruct((frames * ROWS, HEAD), jnp.bfloat16),
            jax.ShapeDtypeStruct((CHUNK, KEYS), jnp.float32),
            jax.ShapeDtypeStruct((ROWS, KEYS, 3 * HEAD), jnp.bfloat16),
        ],
        scratch_shapes=[pltpu.VMEM((ROWS, CHUNK + frames, 3 * HEAD), jnp.bfloat16)],
        compiler_params=pltpu.CompilerParams(vmem_limit_bytes=40 * 1024 * 1024),
        cost_estimate=pl.CostEstimate(flops=2_000_000_000, bytes_accessed=16_000_000, transcendentals=0),
        name="main_part",
    )(bucket_table, bias_table, got)


def first_kernel(bias_ref, halo_ref, own_ref, rest_ref, out_ref, held):
    swap = swap_matrix(PIECE, ROWS, False)
    back = swap_matrix(PIECE, ROWS, True)
    turn_in(held, swap, halo_ref, slice(0, SPAN), 2, KEYS - 2 * CHUNK)
    turn_out(out_ref, back, attend(held, KEYS - CHUNK, bias_ref[...]), 0)


def first_part(bias, halo, own, rest):
    return pl.pallas_call(
        first_kernel,
        in_specs=[VMEM] * 4,
        out_specs=[VMEM] * 2,
        out_shape=[jax.ShapeDtypeStruct(a.shape, a.dtype) for a in (rest, own)],
        input_output_aliases={2: 1, 3: 0},
        compiler_params=pltpu.CompilerParams(vmem_limit_bytes=40 * 1024 * 1024),
        name="first_part",
    )(bias, halo, own, rest)[0]


def exchange(array, groups):
    return lax.all_to_all(array, ("inner", "outer"), 0, 0, tiled=True, axis_index_groups=groups)


def on_device(frames, queries, w_keyval, bucket_table, bias_table, block_mask):
    n_outer = lax.axis_size("outer")
    n_blocks = lax.axis_size("inner") * n_outer
    groups = [list(range(g, g + GROUP)) for g in range(0, n_blocks, GROUP)]
    spatial, width = frames.shape[2:]

    sent = prep(
        frames.reshape(-1, width),
        queries.reshape(-1, queries.shape[3]),
        w_keyval,
        block_mask.reshape(-1),
    )
    got = exchange(sent.reshape(GROUP, MESSAGE, HEAD), groups)
    perm = [(i, (i + GROUP) % n_blocks) for i in range(n_blocks)]
    halo = lax.ppermute(got[GROUP - SPAN :, : 2 * CHUNK, :], ("inner", "outer"), perm)
    rest, bias, own = main_part(bucket_table, bias_table.T, got)
    mixed = first_part(bias, halo, own, rest)
    out = exchange(mixed.reshape(GROUP, CHUNK, HEAD), groups)
    out = out.reshape(spatial // ROWS, HEADS, FR, ROWS, HEAD)
    return out.transpose(2, 0, 3, 1, 4).reshape(queries.shape)


def solution(mesh):
    in_specs = (
        P("outer", "inner", None, None),
        P("outer", "inner", None, None),
        P(),
        P(),
        P(),
        P("outer", "inner", None),
    )
    out_specs = P("outer", "inner", None, None)
    return jax.shard_map(
        on_device, mesh=mesh, in_specs=in_specs, out_specs=out_specs, check_vma=False
    )
```

```python
import jax
import jax.numpy as jnp
from jax import lax
from jax.experimental import pallas as pl
from jax.experimental.pallas import tpu as pltpu
from jax.sharding import PartitionSpec as P

SPAN = 8
HEAD = 128
HEADS = 8
ROWS = 8
GROUP = 64
FR = 6
CHUNK = SPAN * FR
KEYS = 128
MESSAGE = 2 * CHUNK + ROWS
PIECE = 16
SLABS = 4
NEG = -1e30
VMEM = pl.BlockSpec(memory_space=pltpu.VMEM)
SMEM = pl.BlockSpec(memory_space=pltpu.SMEM)


def swap_matrix(frames, rows, back):
    size = frames * rows
    a = lax.broadcasted_iota(jnp.int32, (size, size), 1 if back else 0)
    b = lax.broadcasted_iota(jnp.int32, (size, size), 0 if back else 1)
    hit = b == (a % frames) * rows + a // frames
    return jnp.where(hit, 1.0, 0.0).astype(jnp.bfloat16)


def block_number():
    return lax.axis_index("inner") * lax.axis_size("outer") + lax.axis_index("outer")


def prep_kernel(
    mask_hbm, x_hbm, w_hbm, q_hbm, out_hbm, sent_q_hbm,
    mask_ref, x, w, q, total, out_ref, sent_q, mask_sem, x_sem, w_sem, q_sem, out_sem
):
    depth = w.shape[0] // SLABS
    loads = []
    for slab in range(SLABS):
        span = slice(slab * depth, (slab + 1) * depth)
        loads.append(
            (
                pltpu.make_async_copy(w_hbm.at[span], w.at[span], w_sem.at[slab]),
                pltpu.make_async_copy(x_hbm.at[:, span], x.at[:, span], x_sem.at[slab]),
            )
        )
    q_load = pltpu.make_async_copy(q_hbm, q, q_sem)
    mask_load = pltpu.make_async_copy(mask_hbm, mask_ref, mask_sem)
    for load in loads[0] + loads[1]:
        load.start()
    mask_load.start()
    spatial = x.shape[0] // FR

    def place(to, part, pair, n):
        for half in range(2):
            cols = slice(half * HEAD, (half + 1) * HEAD)
            for group in range(spatial // ROWS):
                at = [f * spatial + group * ROWS for f in range(FR)]
                rows = jnp.concatenate([part[a : a + ROWS, cols] for a in at], axis=0)
                to[group, 2 * pair + half, n * CHUNK : (n + 1) * CHUNK, :] = rows.astype(jnp.bfloat16)

    block = block_number()
    key = lax.broadcasted_iota(jnp.int32, (2 * ROWS, KEYS), 1) - (KEYS - CHUNK)
    reach = block % SPAN - (key + 96 * FR) // FR + 96
    seen = jnp.where(reach == 0, 1.0, 0.0)
    mask_load.wait()
    for m in range(1, SPAN + 1):
        visible = jnp.where((mask_ref[m] == 1) & (block >= m), 1.0, 0.0)
        seen = jnp.where(reach == m, visible, seen)
    seen = seen.astype(jnp.bfloat16)[0:ROWS]
    for group in range(spatial // ROWS):
        for head in range(HEADS):
            out_ref[group, head, 2 * CHUNK :, :] = seen

    for slab in range(SLABS):
        for load in loads[slab]:
            load.wait()
        if slab + 2 < SLABS:
            for load in loads[slab + 2]:
                load.start()
        stores = []
        if slab == 0:
            q_load.start()
        if slab == SLABS - 1:
            q_load.wait()
            for pair in range(HEADS // 2):
                place(sent_q, q[:, pair * 2 * HEAD : (pair + 1) * 2 * HEAD].astype(jnp.float32), pair, 0)
            q_store = pltpu.make_async_copy(sent_q, sent_q_hbm, out_sem.at[HEADS // 2])
            q_store.start()
            stores.append(q_store)
        span = slice(slab * depth, (slab + 1) * depth)
        for pair in range(HEADS // 2):
            for n in range(2):
                first = (n * HEADS + 2 * pair) * HEAD
                cols = slice(first, first + 2 * HEAD)
                part = jnp.dot(x[:, span], w[span, cols], preferred_element_type=jnp.float32)
                if slab > 0:
                    part = part + total[:, cols]
                if slab < SLABS - 1:
                    total[:, cols] = part
                else:
                    place(out_ref, part, pair, n)
            if slab == SLABS - 1:
                heads = slice(2 * pair, 2 * pair + 2)
                store = pltpu.make_async_copy(out_ref.at[:, heads], out_hbm.at[:, heads], out_sem.at[pair])
                store.start()
                stores.append(store)
    for store in stores:
        store.wait()


def prep(frames, queries, w_keyval, block_mask):
    tokens, width = frames.shape
    groups = tokens // FR // ROWS
    any_ = pl.BlockSpec(memory_space=pl.ANY)
    return pl.pallas_call(
        prep_kernel,
        in_specs=[any_] * 4,
        out_specs=[any_] * 2,
        out_shape=[
            jax.ShapeDtypeStruct((groups, HEADS, MESSAGE, HEAD), jnp.bfloat16),
            jax.ShapeDtypeStruct((groups, HEADS, CHUNK, HEAD), jnp.bfloat16),
        ],
        scratch_shapes=[
            pltpu.SMEM(block_mask.shape, block_mask.dtype),
            pltpu.VMEM(frames.shape, jnp.bfloat16),
            pltpu.VMEM(w_keyval.shape, jnp.bfloat16),
            pltpu.VMEM(queries.shape, jnp.bfloat16),
            pltpu.VMEM((tokens, w_keyval.shape[1]), jnp.float32),
            pltpu.VMEM((groups, HEADS, MESSAGE, HEAD), jnp.bfloat16),
            pltpu.VMEM((groups, HEADS, CHUNK, HEAD), jnp.bfloat16),
            pltpu.SemaphoreType.DMA,
            pltpu.SemaphoreType.DMA((SLABS,)),
            pltpu.SemaphoreType.DMA((SLABS,)),
            pltpu.SemaphoreType.DMA,
            pltpu.SemaphoreType.DMA((HEADS // 2 + 1,)),
        ],
        compiler_params=pltpu.CompilerParams(vmem_limit_bytes=58 * 1024 * 1024),
        name="prep",
    )(block_mask, frames, w_keyval, queries)


def bias_of_head(bucket_ref, table_ref):
    head = block_number() % HEADS
    i = lax.broadcasted_iota(jnp.int32, (CHUNK, KEYS), 0)
    key = lax.broadcasted_iota(jnp.int32, (CHUNK, KEYS), 1) - (KEYS - CHUNK)
    off = i - key
    bias = jnp.full((CHUNK, KEYS), NEG, jnp.float32)
    for d in range(bucket_ref.shape[0]):
        bias = jnp.where(off == d, table_ref[head, bucket_ref[d]], bias)
    reach = i // FR - (key + 96 * FR) // FR + 96
    return jnp.where((reach >= 0) & (reach <= SPAN), bias, NEG)


def chunk_bias(base, rows):
    i = lax.broadcasted_iota(jnp.int32, (CHUNK, SPAN * ROWS), 0)
    b = lax.broadcasted_iota(jnp.int32, (CHUNK, SPAN * ROWS), 1)
    spread = jnp.where(i // FR * ROWS == b, 1.0, 0.0).astype(jnp.bfloat16)
    rows = rows.astype(jnp.float32).reshape(SPAN * ROWS, KEYS).astype(jnp.bfloat16)
    seen = jnp.dot(spread, rows, preferred_element_type=jnp.float32)
    return jnp.where(seen > 0.5, base, NEG)


def score(held, queries, start, at, bias):
    first = start + CHUNK - KEYS
    scores = []
    for s in range(0, ROWS, 2):
        q = jnp.concatenate([queries[t, at : at + CHUNK, :] for t in (s, s + 1)], axis=0)
        k = jnp.concatenate([held[t, first : first + KEYS, 0:HEAD] for t in (s, s + 1)], axis=0)
        both = lax.dot_general(q, k, (((1,), (1,)), ((), ())), preferred_element_type=jnp.float32)
        scores += [both[0:CHUNK, 0:KEYS], both[CHUNK:, KEYS:]]
    return jnp.stack(scores, axis=0) * (HEAD**-0.5) + bias[None]


def mix(held, start, scores):
    first = start + CHUNK - KEYS
    expo = jnp.exp(scores - jnp.max(scores, axis=2, keepdims=True))
    weights = expo * (1.0 / jnp.sum(expo, axis=2, keepdims=True))
    weights = weights.astype(jnp.bfloat16)
    mixed = []
    for s in range(0, ROWS, 2):
        v = jnp.concatenate([held[t, first : first + KEYS, HEAD : 2 * HEAD] for t in (s, s + 1)], axis=1)
        both = jnp.dot(weights[s : s + 2].reshape(2 * CHUNK, KEYS), v, preferred_element_type=jnp.float32)
        both = both.astype(jnp.bfloat16)
        mixed += [both[0:CHUNK, 0:HEAD], both[CHUNK:, HEAD:]]
    return mixed


def turn_in(held, swap, parts, at):
    rows = jnp.concatenate([part.reshape(CHUNK * ROWS, HEAD) for part in parts], axis=1)
    for piece in range(CHUNK // PIECE):
        part = rows[piece * PIECE * ROWS : (piece + 1) * PIECE * ROWS]
        turned = jnp.dot(swap, part, preferred_element_type=jnp.float32).astype(jnp.bfloat16)
        start = at + piece * PIECE
        held[:, start : start + PIECE, :] = turned.reshape(ROWS, PIECE, len(parts) * HEAD)


def turn_out(out_ref, back, mixed, at):
    for piece in range(CHUNK // PIECE):
        rows = [m[piece * PIECE : (piece + 1) * PIECE] for m in mixed]
        rows = jnp.concatenate(rows, axis=0)
        start = at + piece * PIECE * ROWS
        out_ref[start : start + PIECE * ROWS, :] = jnp.dot(
            back, rows, preferred_element_type=jnp.float32
        ).astype(jnp.bfloat16)


LEAD = KEYS - CHUNK
CHUNKS = GROUP // SPAN


def keyval_kernel(bucket_ref, table_ref, got_ref, held, bias_ref):
    swap = swap_matrix(PIECE, ROWS, False)
    held[:, 0:LEAD, :] = jnp.zeros((ROWS, LEAD, 2 * HEAD), jnp.bfloat16)
    base = bias_of_head(bucket_ref, table_ref)
    for chunk in range(CHUNKS):
        blocks = slice(chunk * SPAN, (chunk + 1) * SPAN)
        parts = [got_ref[blocks, n * CHUNK : (n + 1) * CHUNK, :] for n in range(2)]
        turn_in(held, swap, parts, LEAD + chunk * CHUNK)
        bias_ref[chunk] = chunk_bias(base, got_ref[blocks, 2 * CHUNK :, :])


def keyval_part(bucket_table, bias_table, got):
    return pl.pallas_call(
        keyval_kernel,
        in_specs=[SMEM, SMEM, VMEM],
        out_specs=[VMEM] * 2,
        out_shape=[
            jax.ShapeDtypeStruct((ROWS, LEAD + GROUP * FR, 2 * HEAD), jnp.bfloat16),
            jax.ShapeDtypeStruct((CHUNKS, CHUNK, KEYS), jnp.float32),
        ],
        compiler_params=pltpu.CompilerParams(vmem_limit_bytes=40 * 1024 * 1024),
        cost_estimate=pl.CostEstimate(flops=1_000_000_000, bytes_accessed=4_000_000, transcendentals=0),
        name="keyval_part",
    )(bucket_table, bias_table, got)


def attention_kernel(held_in, bias_ref, halo_ref, got_ref, out_ref, held, queries):
    swap = swap_matrix(PIECE, ROWS, False)
    back = swap_matrix(PIECE, ROWS, True)
    held[:, LEAD - CHUNK : LEAD, :] = halo_ref[...]
    for chunk in range(CHUNKS):
        turn_in(queries, swap, [got_ref[chunk * SPAN : (chunk + 1) * SPAN]], chunk * CHUNK)

    def score_of(chunk):
        return score(held, queries, LEAD + chunk * CHUNK, chunk * CHUNK, bias_ref[chunk])

    scores = score_of(0)
    mixed = None
    for chunk in range(CHUNKS):
        after = score_of(chunk + 1) if chunk + 1 < CHUNKS else None
        if mixed is not None:
            turn_out(out_ref, back, mixed, (chunk - 1) * CHUNK * ROWS)
        mixed = mix(held, LEAD + chunk * CHUNK, scores)
        scores = after
    turn_out(out_ref, back, mixed, (CHUNKS - 1) * CHUNK * ROWS)


def attention_part(held, bias, halo, got):
    return pl.pallas_call(
        attention_kernel,
        in_specs=[VMEM] * 4,
        out_specs=[VMEM] * 2,
        out_shape=[
            jax.ShapeDtypeStruct((GROUP * FR * ROWS, HEAD), jnp.bfloat16),
            jax.ShapeDtypeStruct(held.shape, held.dtype),
        ],
        scratch_shapes=[pltpu.VMEM((ROWS, GROUP * FR, HEAD), jnp.bfloat16)],
        input_output_aliases={0: 1},
        compiler_params=pltpu.CompilerParams(vmem_limit_bytes=40 * 1024 * 1024),
        name="attention_part",
    )(held, bias, halo, got)[0]


def exchange(array, groups):
    return lax.all_to_all(array, ("inner", "outer"), 0, 0, tiled=True, axis_index_groups=groups)


def on_device(frames, queries, w_keyval, bucket_table, bias_table, block_mask):
    n_outer = lax.axis_size("outer")
    n_blocks = lax.axis_size("inner") * n_outer
    groups = [list(range(g, g + GROUP)) for g in range(0, n_blocks, GROUP)]
    spatial, width = frames.shape[2:]

    sent_kv, sent_q = prep(
        frames.reshape(-1, width),
        queries.reshape(-1, queries.shape[3]),
        w_keyval,
        block_mask.reshape(-1),
    )
    got_kv = exchange(sent_kv.reshape(GROUP, MESSAGE, HEAD), groups)
    got_q = exchange(sent_q.reshape(GROUP, CHUNK, HEAD), groups)
    held, bias = keyval_part(bucket_table, bias_table.T, got_kv)
    perm = [(i, (i + GROUP) % n_blocks) for i in range(n_blocks)]
    halo = lax.ppermute(held[:, -CHUNK:, :], ("inner", "outer"), perm)
    mixed = attention_part(held, bias, halo, got_q)
    out = exchange(mixed.reshape(GROUP, CHUNK, HEAD), groups)
    out = out.reshape(spatial // ROWS, HEADS, FR, ROWS, HEAD)
    return out.transpose(2, 0, 3, 1, 4).reshape(queries.shape)


def solution(mesh):
    in_specs = (
        P("outer", "inner", None, None),
        P("outer", "inner", None, None),
        P(),
        P(),
        P(),
        P("outer", "inner", None),
    )
    out_specs = P("outer", "inner", None, None)
    return jax.shard_map(
        on_device, mesh=mesh, in_specs=in_specs, out_specs=out_specs, check_vma=False
    )
```

```python
import jax
import jax.numpy as jnp
from jax import lax
from jax.experimental import pallas as pl
from jax.experimental.pallas import tpu as pltpu
from jax.sharding import PartitionSpec as P

SPAN = 8
HEAD = 128
HEADS = 8
ROWS = 8
GROUP = 64
FR = 6
CHUNK = SPAN * FR
KEYS = 128
MESSAGE = 3 * CHUNK + ROWS
PIECE = 16
SLABS = 4
NEG = -1e30
VMEM = pl.BlockSpec(memory_space=pltpu.VMEM)
SMEM = pl.BlockSpec(memory_space=pltpu.SMEM)


def swap_matrix(frames, rows, back):
    size = frames * rows
    a = lax.broadcasted_iota(jnp.int32, (size, size), 1 if back else 0)
    b = lax.broadcasted_iota(jnp.int32, (size, size), 0 if back else 1)
    hit = b == (a % frames) * rows + a // frames
    return jnp.where(hit, 1.0, 0.0).astype(jnp.bfloat16)


def block_number():
    return lax.axis_index("inner") * lax.axis_size("outer") + lax.axis_index("outer")


def prep_kernel(
    mask_hbm, x_hbm, w_hbm, q_hbm, out_hbm, mask_ref, x, w, q, total, out_ref, mask_sem, x_sem, w_sem, q_sem, out_sem
):
    depth = w.shape[0] // SLABS
    loads = []
    for slab in range(SLABS):
        span = slice(slab * depth, (slab + 1) * depth)
        loads.append(
            (
                pltpu.make_async_copy(w_hbm.at[span], w.at[span], w_sem.at[slab]),
                pltpu.make_async_copy(x_hbm.at[:, span], x.at[:, span], x_sem.at[slab]),
            )
        )
    q_load = pltpu.make_async_copy(q_hbm, q, q_sem)
    mask_load = pltpu.make_async_copy(mask_hbm, mask_ref, mask_sem)
    for load in loads[0] + loads[1]:
        load.start()
    mask_load.start()
    spatial = x.shape[0] // FR

    def place(part, pair, n):
        for half in range(2):
            cols = slice(half * HEAD, (half + 1) * HEAD)
            for group in range(spatial // ROWS):
                at = [f * spatial + group * ROWS for f in range(FR)]
                rows = jnp.concatenate([part[a : a + ROWS, cols] for a in at], axis=0)
                out_ref[group, 2 * pair + half, n * CHUNK : (n + 1) * CHUNK, :] = rows.astype(jnp.bfloat16)

    block = block_number()
    key = lax.broadcasted_iota(jnp.int32, (2 * ROWS, KEYS), 1) - (KEYS - CHUNK)
    reach = block % SPAN - (key + 96 * FR) // FR + 96
    seen = jnp.where(reach == 0, 1.0, 0.0)
    mask_load.wait()
    for m in range(1, SPAN + 1):
        visible = jnp.where((mask_ref[m] == 1) & (block >= m), 1.0, 0.0)
        seen = jnp.where(reach == m, visible, seen)
    seen = seen.astype(jnp.bfloat16)[0:ROWS]
    for group in range(spatial // ROWS):
        for head in range(HEADS):
            out_ref[group, head, 3 * CHUNK :, :] = seen

    for slab in range(SLABS):
        for load in loads[slab]:
            load.wait()
        if slab + 2 < SLABS:
            for load in loads[slab + 2]:
                load.start()
        if slab == 0:
            q_load.start()
        if slab == SLABS - 1:
            q_load.wait()
            for pair in range(HEADS // 2):
                place(q[:, pair * 2 * HEAD : (pair + 1) * 2 * HEAD].astype(jnp.float32), pair, 2)
        span = slice(slab * depth, (slab + 1) * depth)
        stores = []
        for pair in range(HEADS // 2):
            for n in range(2):
                first = (n * HEADS + 2 * pair) * HEAD
                cols = slice(first, first + 2 * HEAD)
                part = jnp.dot(x[:, span], w[span, cols], preferred_element_type=jnp.float32)
                if slab > 0:
                    part = part + total[:, cols]
                if slab < SLABS - 1:
                    total[:, cols] = part
                else:
                    place(part, pair, n)
            if slab == SLABS - 1:
                heads = slice(2 * pair, 2 * pair + 2)
                store = pltpu.make_async_copy(out_ref.at[:, heads], out_hbm.at[:, heads], out_sem.at[pair])
                store.start()
                stores.append(store)
    for store in stores:
        store.wait()


def prep(frames, queries, w_keyval, block_mask):
    tokens, width = frames.shape
    groups = tokens // FR // ROWS
    any_ = pl.BlockSpec(memory_space=pl.ANY)
    return pl.pallas_call(
        prep_kernel,
        in_specs=[any_] * 4,
        out_specs=any_,
        out_shape=jax.ShapeDtypeStruct((groups, HEADS, MESSAGE, HEAD), jnp.bfloat16),
        scratch_shapes=[
            pltpu.SMEM(block_mask.shape, block_mask.dtype),
            pltpu.VMEM(frames.shape, jnp.bfloat16),
            pltpu.VMEM(w_keyval.shape, jnp.bfloat16),
            pltpu.VMEM(queries.shape, jnp.bfloat16),
            pltpu.VMEM((tokens, w_keyval.shape[1]), jnp.float32),
            pltpu.VMEM((groups, HEADS, MESSAGE, HEAD), jnp.bfloat16),
            pltpu.SemaphoreType.DMA,
            pltpu.SemaphoreType.DMA((SLABS,)),
            pltpu.SemaphoreType.DMA((SLABS,)),
            pltpu.SemaphoreType.DMA,
            pltpu.SemaphoreType.DMA((HEADS // 2,)),
        ],
        compiler_params=pltpu.CompilerParams(vmem_limit_bytes=58 * 1024 * 1024),
        name="prep",
    )(block_mask, frames, w_keyval, queries)


def bias_of_head(bucket_ref, table_ref):
    head = block_number() % HEADS
    i = lax.broadcasted_iota(jnp.int32, (CHUNK, KEYS), 0)
    key = lax.broadcasted_iota(jnp.int32, (CHUNK, KEYS), 1) - (KEYS - CHUNK)
    off = i - key
    bias = jnp.full((CHUNK, KEYS), NEG, jnp.float32)
    for d in range(bucket_ref.shape[0]):
        bias = jnp.where(off == d, table_ref[head, bucket_ref[d]], bias)
    reach = i // FR - (key + 96 * FR) // FR + 96
    return jnp.where((reach >= 0) & (reach <= SPAN), bias, NEG)


def chunk_bias(base, rows):
    i = lax.broadcasted_iota(jnp.int32, (CHUNK, SPAN * ROWS), 0)
    b = lax.broadcasted_iota(jnp.int32, (CHUNK, SPAN * ROWS), 1)
    spread = jnp.where(i // FR * ROWS == b, 1.0, 0.0).astype(jnp.bfloat16)
    rows = rows.astype(jnp.float32).reshape(SPAN * ROWS, KEYS).astype(jnp.bfloat16)
    seen = jnp.dot(spread, rows, preferred_element_type=jnp.float32)
    return jnp.where(seen > 0.5, base, NEG)


def score(held, start, bias, tokens=range(ROWS)):
    first = start + CHUNK - KEYS
    scores = []
    for s in tokens[::2]:
        q = jnp.concatenate([held[t, start : start + CHUNK, 2 * HEAD :] for t in (s, s + 1)], axis=0)
        k = jnp.concatenate([held[t, first : first + KEYS, 0:HEAD] for t in (s, s + 1)], axis=0)
        both = lax.dot_general(q, k, (((1,), (1,)), ((), ())), preferred_element_type=jnp.float32)
        scores += [both[0:CHUNK, 0:KEYS], both[CHUNK:, KEYS:]]
    return jnp.stack(scores, axis=0) * (HEAD**-0.5) + bias[None]


def mix(held, start, scores, tokens=range(ROWS)):
    first = start + CHUNK - KEYS
    expo = jnp.exp(scores - jnp.max(scores, axis=2, keepdims=True))
    weights = expo * (1.0 / jnp.sum(expo, axis=2, keepdims=True))
    weights = weights.astype(jnp.bfloat16)
    mixed = []
    for n, s in enumerate(tokens[::2]):
        v = jnp.concatenate([held[t, first : first + KEYS, HEAD : 2 * HEAD] for t in (s, s + 1)], axis=1)
        both = jnp.dot(weights[2 * n : 2 * n + 2].reshape(2 * CHUNK, KEYS), v, preferred_element_type=jnp.float32)
        both = both.astype(jnp.bfloat16)
        mixed += [both[0:CHUNK, 0:HEAD], both[CHUNK:, HEAD:]]
    return mixed


def attend(held, start, bias):
    return mix(held, start, score(held, start, bias))


def turn_in(held, swap, got_ref, blocks, parts, at):
    rows = [
        got_ref[blocks, n * CHUNK : (n + 1) * CHUNK, :].reshape(CHUNK * ROWS, HEAD) for n in range(parts)
    ]
    rows = jnp.concatenate(rows, axis=1)
    for piece in range(CHUNK // PIECE):
        part = rows[piece * PIECE * ROWS : (piece + 1) * PIECE * ROWS]
        turned = jnp.dot(swap, part, preferred_element_type=jnp.float32).astype(jnp.bfloat16)
        start = at + piece * PIECE
        held[:, start : start + PIECE, 0 : parts * HEAD] = turned.reshape(ROWS, PIECE, parts * HEAD)


def turn_out(out_ref, back, mixed, at):
    for piece in range(CHUNK // PIECE):
        rows = [m[piece * PIECE : (piece + 1) * PIECE] for m in mixed]
        rows = jnp.concatenate(rows, axis=0)
        start = at + piece * PIECE * ROWS
        out_ref[start : start + PIECE * ROWS, :] = jnp.dot(
            back, rows, preferred_element_type=jnp.float32
        ).astype(jnp.bfloat16)


def main_kernel(bucket_ref, table_ref, got_ref, out_ref, bias_ref, first_ref, held):
    base = bias_of_head(bucket_ref, table_ref)
    swap = swap_matrix(PIECE, ROWS, False)
    back = swap_matrix(PIECE, ROWS, True)
    lead = CHUNK
    held[:, 0:lead, :] = jnp.zeros((ROWS, lead, 3 * HEAD), jnp.bfloat16)
    for chunk in range(GROUP // SPAN):
        turn_in(held, swap, got_ref, slice(chunk * SPAN, (chunk + 1) * SPAN), 3, lead + chunk * CHUNK)

    def bias_of(chunk):
        return chunk_bias(base, got_ref[chunk * SPAN : (chunk + 1) * SPAN, 3 * CHUNK :, :])

    bias_ref[...] = bias_of(0)
    first_ref[:, : KEYS - CHUNK, :] = jnp.zeros((ROWS, KEYS - CHUNK, 3 * HEAD), jnp.bfloat16)
    first_ref[:, KEYS - CHUNK :, :] = held[:, lead : lead + CHUNK, :]
    chunks = GROUP // SPAN
    scores = score(held, lead + CHUNK, bias_of(1))
    mixed = None
    for chunk in range(1, chunks):
        after = None
        if chunk + 1 < chunks:
            after = score(held, lead + (chunk + 1) * CHUNK, bias_of(chunk + 1))
        if mixed is not None:
            turn_out(out_ref, back, mixed, (chunk - 1) * CHUNK * ROWS)
        mixed = mix(held, lead + chunk * CHUNK, scores)
        scores = after
    turn_out(out_ref, back, mixed, (chunks - 1) * CHUNK * ROWS)


def main_part(bucket_table, bias_table, got):
    frames = GROUP * FR
    return pl.pallas_call(
        main_kernel,
        in_specs=[SMEM, SMEM, VMEM],
        out_specs=[VMEM] * 3,
        out_shape=[
            jax.ShapeDtypeStruct((frames * ROWS, HEAD), jnp.bfloat16),
            jax.ShapeDtypeStruct((CHUNK, KEYS), jnp.float32),
            jax.ShapeDtypeStruct((ROWS, KEYS, 3 * HEAD), jnp.bfloat16),
        ],
        scratch_shapes=[pltpu.VMEM((ROWS, CHUNK + frames, 3 * HEAD), jnp.bfloat16)],
        compiler_params=pltpu.CompilerParams(vmem_limit_bytes=40 * 1024 * 1024),
        cost_estimate=pl.CostEstimate(flops=2_000_000_000, bytes_accessed=16_000_000, transcendentals=0),
        name="main_part",
    )(bucket_table, bias_table, got)


def first_kernel(bias_ref, halo_ref, own_ref, rest_ref, out_ref, held):
    swap = swap_matrix(PIECE, ROWS, False)
    back = swap_matrix(PIECE, ROWS, True)
    turn_in(held, swap, halo_ref, slice(0, SPAN), 2, KEYS - 2 * CHUNK)
    bias = bias_ref[...]
    halves = [range(0, ROWS // 2), range(ROWS // 2, ROWS)]
    scores = [score(held, KEYS - CHUNK, bias, tokens) for tokens in halves]
    mixed = [mix(held, KEYS - CHUNK, part, tokens) for part, tokens in zip(scores, halves)]
    turn_out(out_ref, back, mixed[0] + mixed[1], 0)


def first_part(bias, halo, own, rest):
    return pl.pallas_call(
        first_kernel,
        in_specs=[VMEM] * 4,
        out_specs=[VMEM] * 2,
        out_shape=[jax.ShapeDtypeStruct(a.shape, a.dtype) for a in (rest, own)],
        input_output_aliases={2: 1, 3: 0},
        compiler_params=pltpu.CompilerParams(vmem_limit_bytes=40 * 1024 * 1024),
        name="first_part",
    )(bias, halo, own, rest)[0]


def unpack_kernel(got_ref, out_hbm, out_ref, sems):
    stores = []
    for two in range(FR // 2):
        for head in range(HEADS):
            tiles = [
                got_ref[group * HEADS + head, two * 2 * ROWS : (two + 1) * 2 * ROWS, :].astype(jnp.float32)
                for group in range(got_ref.shape[0] // HEADS)
            ]
            for half in range(2):
                rows = jnp.concatenate([t[half * ROWS : (half + 1) * ROWS] for t in tiles], axis=0)
                out_ref[2 * two + half, :, head * HEAD : (head + 1) * HEAD] = rows.astype(jnp.bfloat16)
        span = slice(2 * two, 2 * two + 2)
        store = pltpu.make_async_copy(out_ref.at[span], out_hbm.at[span], sems.at[two])
        store.start()
        stores.append(store)
    for store in stores:
        store.wait()


def unpack(got):
    shape = (FR, got.shape[0] // HEADS * ROWS, HEADS * HEAD)
    return pl.pallas_call(
        unpack_kernel,
        in_specs=[VMEM],
        out_specs=pl.BlockSpec(memory_space=pl.ANY),
        out_shape=jax.ShapeDtypeStruct(shape, got.dtype),
        scratch_shapes=[pltpu.VMEM(shape, jnp.bfloat16), pltpu.SemaphoreType.DMA((FR // 2,))],
        compiler_params=pltpu.CompilerParams(vmem_limit_bytes=40 * 1024 * 1024),
        name="unpack",
    )(got)


def exchange(array, groups):
    return lax.all_to_all(array, ("inner", "outer"), 0, 0, tiled=True, axis_index_groups=groups)


def on_device(frames, queries, w_keyval, bucket_table, bias_table, block_mask):
    n_outer = lax.axis_size("outer")
    n_blocks = lax.axis_size("inner") * n_outer
    groups = [list(range(g, g + GROUP)) for g in range(0, n_blocks, GROUP)]
    width = frames.shape[3]

    sent = prep(
        frames.reshape(-1, width),
        queries.reshape(-1, queries.shape[3]),
        w_keyval,
        block_mask.reshape(-1),
    )
    got = exchange(sent.reshape(GROUP, MESSAGE, HEAD), groups)
    perm = [(i, i + GROUP) for i in range(n_blocks - GROUP)]
    halo = lax.ppermute(got[GROUP - SPAN :, : 2 * CHUNK, :], ("inner", "outer"), perm)
    rest, bias, own = main_part(bucket_table, bias_table.T, got)
    mixed = first_part(bias, halo, own, rest)
    out = exchange(mixed.reshape(GROUP, CHUNK, HEAD), groups)
    return unpack(out).reshape(queries.shape)


def solution(mesh):
    in_specs = (
        P("outer", "inner", None, None),
        P("outer", "inner", None, None),
        P(),
        P(),
        P(),
        P("outer", "inner", None),
    )
    out_specs = P("outer", "inner", None, None)
    return jax.shard_map(
        on_device, mesh=mesh, in_specs=in_specs, out_specs=out_specs, check_vma=False
    )
```

```python
import jax
import jax.numpy as jnp
from jax import lax
from jax.experimental import pallas as pl
from jax.experimental.pallas import tpu as pltpu
from jax.sharding import PartitionSpec as P

SPAN = 8
HEAD = 128
HEADS = 8
ROWS = 8
GROUP = 64
FR = 6
CHUNK = SPAN * FR
KEYS = 128
MESSAGE = 3 * CHUNK + ROWS
PIECE = 16
SLABS = 4
NEG = -1e30
VMEM = pl.BlockSpec(memory_space=pltpu.VMEM)
SMEM = pl.BlockSpec(memory_space=pltpu.SMEM)


def swap_matrix(frames, rows, back):
    size = frames * rows
    a = lax.broadcasted_iota(jnp.int32, (size, size), 1 if back else 0)
    b = lax.broadcasted_iota(jnp.int32, (size, size), 0 if back else 1)
    hit = b == (a % frames) * rows + a // frames
    return jnp.where(hit, 1.0, 0.0).astype(jnp.bfloat16)


def block_number():
    return lax.axis_index("inner") * lax.axis_size("outer") + lax.axis_index("outer")


def prep_kernel(
    mask_hbm, x_hbm, w_hbm, q_hbm, out_hbm, mask_ref, x, w, q, total, out_ref, mask_sem, x_sem, w_sem, q_sem, out_sem
):
    depth = w.shape[0] // SLABS
    loads = []
    for slab in range(SLABS):
        span = slice(slab * depth, (slab + 1) * depth)
        loads.append(
            (
                pltpu.make_async_copy(w_hbm.at[span], w.at[span], w_sem.at[slab]),
                pltpu.make_async_copy(x_hbm.at[:, span], x.at[:, span], x_sem.at[slab]),
            )
        )
    q_load = pltpu.make_async_copy(q_hbm, q, q_sem)
    mask_load = pltpu.make_async_copy(mask_hbm, mask_ref, mask_sem)
    for slab in range(2):
        for load in loads[slab]:
            load.start(priority=slab)
    mask_load.start()
    spatial = x.shape[0] // FR

    def place(part, pair, n):
        for half in range(2):
            cols = slice(half * HEAD, (half + 1) * HEAD)
            for group in range(spatial // ROWS):
                at = [f * spatial + group * ROWS for f in range(FR)]
                rows = jnp.concatenate([part[a : a + ROWS, cols] for a in at], axis=0)
                out_ref[group, 2 * pair + half, n * CHUNK : (n + 1) * CHUNK, :] = rows.astype(jnp.bfloat16)

    block = block_number()
    key = lax.broadcasted_iota(jnp.int32, (2 * ROWS, KEYS), 1) - (KEYS - CHUNK)
    reach = block % SPAN - (key + 96 * FR) // FR + 96
    seen = jnp.where(reach == 0, 1.0, 0.0)
    mask_load.wait()
    for m in range(1, SPAN + 1):
        visible = jnp.where((mask_ref[m] == 1) & (block >= m), 1.0, 0.0)
        seen = jnp.where(reach == m, visible, seen)
    seen = seen.astype(jnp.bfloat16)[0:ROWS]
    for group in range(spatial // ROWS):
        for head in range(HEADS):
            out_ref[group, head, 3 * CHUNK :, :] = seen

    for slab in range(SLABS):
        for load in loads[slab]:
            load.wait()
        if slab + 2 < SLABS:
            for load in loads[slab + 2]:
                load.start(priority=slab % 2)
        if slab == 0:
            q_load.start()
        if slab == SLABS - 1:
            q_load.wait()
            for pair in range(HEADS // 2):
                place(q[:, pair * 2 * HEAD : (pair + 1) * 2 * HEAD].astype(jnp.float32), pair, 2)
        span = slice(slab * depth, (slab + 1) * depth)
        stores = []
        for pair in range(HEADS // 2):
            for n in range(2):
                first = (n * HEADS + 2 * pair) * HEAD
                cols = slice(first, first + 2 * HEAD)
                part = jnp.dot(x[:, span], w[span, cols], preferred_element_type=jnp.float32)
                if slab > 0:
                    part = part + total[:, cols]
                if slab < SLABS - 1:
                    total[:, cols] = part
                else:
                    place(part, pair, n)
            if slab == SLABS - 1:
                heads = slice(2 * pair, 2 * pair + 2)
                store = pltpu.make_async_copy(out_ref.at[:, heads], out_hbm.at[:, heads], out_sem.at[pair])
                store.start()
                stores.append(store)
    for store in stores:
        store.wait()


def prep(frames, queries, w_keyval, block_mask):
    tokens, width = frames.shape
    groups = tokens // FR // ROWS
    any_ = pl.BlockSpec(memory_space=pl.ANY)
    return pl.pallas_call(
        prep_kernel,
        in_specs=[any_] * 4,
        out_specs=any_,
        out_shape=jax.ShapeDtypeStruct((groups, HEADS, MESSAGE, HEAD), jnp.bfloat16),
        scratch_shapes=[
            pltpu.SMEM(block_mask.shape, block_mask.dtype),
            pltpu.VMEM(frames.shape, jnp.bfloat16),
            pltpu.VMEM(w_keyval.shape, jnp.bfloat16),
            pltpu.VMEM(queries.shape, jnp.bfloat16),
            pltpu.VMEM((tokens, w_keyval.shape[1]), jnp.float32),
            pltpu.VMEM((groups, HEADS, MESSAGE, HEAD), jnp.bfloat16),
            pltpu.SemaphoreType.DMA,
            pltpu.SemaphoreType.DMA((SLABS,)),
            pltpu.SemaphoreType.DMA((SLABS,)),
            pltpu.SemaphoreType.DMA,
            pltpu.SemaphoreType.DMA((HEADS // 2,)),
        ],
        compiler_params=pltpu.CompilerParams(vmem_limit_bytes=58 * 1024 * 1024),
        name="prep",
    )(block_mask, frames, w_keyval, queries)


def bias_of_head(bucket_ref, table_ref):
    head = block_number() % HEADS
    i = lax.broadcasted_iota(jnp.int32, (CHUNK, KEYS), 0)
    key = lax.broadcasted_iota(jnp.int32, (CHUNK, KEYS), 1) - (KEYS - CHUNK)
    off = i - key
    bias = jnp.full((CHUNK, KEYS), NEG, jnp.float32)
    for d in range(bucket_ref.shape[0]):
        bias = jnp.where(off == d, table_ref[head, bucket_ref[d]], bias)
    reach = i // FR - (key + 96 * FR) // FR + 96
    return jnp.where((reach >= 0) & (reach <= SPAN), bias, NEG)


def chunk_bias(base, rows):
    i = lax.broadcasted_iota(jnp.int32, (CHUNK, SPAN * ROWS), 0)
    b = lax.broadcasted_iota(jnp.int32, (CHUNK, SPAN * ROWS), 1)
    spread = jnp.where(i // FR * ROWS == b, 1.0, 0.0).astype(jnp.bfloat16)
    rows = rows.astype(jnp.float32).reshape(SPAN * ROWS, KEYS).astype(jnp.bfloat16)
    seen = jnp.dot(spread, rows, preferred_element_type=jnp.float32)
    return jnp.where(seen > 0.5, base, NEG)


def score(held, start, bias, tokens=range(ROWS)):
    first = start + CHUNK - KEYS
    scores = []
    for s in tokens[::2]:
        q = jnp.concatenate([held[t, start : start + CHUNK, 2 * HEAD :] for t in (s, s + 1)], axis=0)
        k = jnp.concatenate([held[t, first : first + KEYS, 0:HEAD] for t in (s, s + 1)], axis=0)
        both = lax.dot_general(q, k, (((1,), (1,)), ((), ())), preferred_element_type=jnp.float32)
        scores += [both[0:CHUNK, 0:KEYS], both[CHUNK:, KEYS:]]
    return jnp.stack(scores, axis=0) * (HEAD**-0.5) + bias[None]


def mix(held, start, scores, tokens=range(ROWS)):
    first = start + CHUNK - KEYS
    expo = jnp.exp(scores - jnp.max(scores, axis=2, keepdims=True))
    weights = expo * (1.0 / jnp.sum(expo, axis=2, keepdims=True))
    weights = weights.astype(jnp.bfloat16)
    mixed = []
    for n, s in enumerate(tokens[::2]):
        v = jnp.concatenate([held[t, first : first + KEYS, HEAD : 2 * HEAD] for t in (s, s + 1)], axis=1)
        both = jnp.dot(weights[2 * n : 2 * n + 2].reshape(2 * CHUNK, KEYS), v, preferred_element_type=jnp.float32)
        both = both.astype(jnp.bfloat16)
        mixed += [both[0:CHUNK, 0:HEAD], both[CHUNK:, HEAD:]]
    return mixed


def attend(held, start, bias):
    return mix(held, start, score(held, start, bias))


def turn_in(held, swap, got_ref, blocks, parts, at):
    rows = [
        got_ref[blocks, n * CHUNK : (n + 1) * CHUNK, :].reshape(CHUNK * ROWS, HEAD) for n in range(parts)
    ]
    rows = jnp.concatenate(rows, axis=1)
    for piece in range(CHUNK // PIECE):
        part = rows[piece * PIECE * ROWS : (piece + 1) * PIECE * ROWS]
        turned = jnp.dot(swap, part, preferred_element_type=jnp.float32).astype(jnp.bfloat16)
        start = at + piece * PIECE
        held[:, start : start + PIECE, 0 : parts * HEAD] = turned.reshape(ROWS, PIECE, parts * HEAD)


def turn_out(out_ref, back, mixed, at):
    for piece in range(CHUNK // PIECE):
        rows = [m[piece * PIECE : (piece + 1) * PIECE] for m in mixed]
        rows = jnp.concatenate(rows, axis=0)
        start = at + piece * PIECE * ROWS
        out_ref[start : start + PIECE * ROWS, :] = jnp.dot(
            back, rows, preferred_element_type=jnp.float32
        ).astype(jnp.bfloat16)


def main_kernel(bucket_ref, table_ref, got_ref, out_ref, bias_ref, first_ref, held):
    base = bias_of_head(bucket_ref, table_ref)
    swap = swap_matrix(PIECE, ROWS, False)
    back = swap_matrix(PIECE, ROWS, True)
    lead = CHUNK
    held[:, 0:lead, :] = jnp.zeros((ROWS, lead, 3 * HEAD), jnp.bfloat16)
    for chunk in range(GROUP // SPAN):
        turn_in(held, swap, got_ref, slice(chunk * SPAN, (chunk + 1) * SPAN), 3, lead + chunk * CHUNK)

    def bias_of(chunk):
        return chunk_bias(base, got_ref[chunk * SPAN : (chunk + 1) * SPAN, 3 * CHUNK :, :])

    bias_ref[...] = bias_of(0)
    first_ref[:, : KEYS - CHUNK, :] = jnp.zeros((ROWS, KEYS - CHUNK, 3 * HEAD), jnp.bfloat16)
    first_ref[:, KEYS - CHUNK :, :] = held[:, lead : lead + CHUNK, :]
    chunks = GROUP // SPAN
    scores = score(held, lead + CHUNK, bias_of(1))
    mixed = None
    for chunk in range(1, chunks):
        after = None
        if chunk + 1 < chunks:
            after = score(held, lead + (chunk + 1) * CHUNK, bias_of(chunk + 1))
        if mixed is not None:
            turn_out(out_ref, back, mixed, (chunk - 1) * CHUNK * ROWS)
        mixed = mix(held, lead + chunk * CHUNK, scores)
        scores = after
    turn_out(out_ref, back, mixed, (chunks - 1) * CHUNK * ROWS)


def main_part(bucket_table, bias_table, got):
    frames = GROUP * FR
    return pl.pallas_call(
        main_kernel,
        in_specs=[SMEM, SMEM, VMEM],
        out_specs=[VMEM] * 3,
        out_shape=[
            jax.ShapeDtypeStruct((frames * ROWS, HEAD), jnp.bfloat16),
            jax.ShapeDtypeStruct((CHUNK, KEYS), jnp.float32),
            jax.ShapeDtypeStruct((ROWS, KEYS, 3 * HEAD), jnp.bfloat16),
        ],
        scratch_shapes=[pltpu.VMEM((ROWS, CHUNK + frames, 3 * HEAD), jnp.bfloat16)],
        compiler_params=pltpu.CompilerParams(vmem_limit_bytes=40 * 1024 * 1024),
        cost_estimate=pl.CostEstimate(flops=2_000_000_000, bytes_accessed=16_000_000, transcendentals=0),
        name="main_part",
    )(bucket_table, bias_table, got)


def first_kernel(bias_ref, halo_ref, own_ref, rest_ref, out_ref, held):
    swap = swap_matrix(PIECE, ROWS, False)
    back = swap_matrix(PIECE, ROWS, True)
    turn_in(held, swap, halo_ref, slice(0, SPAN), 2, KEYS - 2 * CHUNK)
    bias = bias_ref[...]
    halves = [range(0, ROWS // 2), range(ROWS // 2, ROWS)]
    scores = [score(held, KEYS - CHUNK, bias, tokens) for tokens in halves]
    mixed = [mix(held, KEYS - CHUNK, part, tokens) for part, tokens in zip(scores, halves)]
    turn_out(out_ref, back, mixed[0] + mixed[1], 0)


def first_part(bias, halo, own, rest):
    return pl.pallas_call(
        first_kernel,
        in_specs=[VMEM] * 4,
        out_specs=[VMEM] * 2,
        out_shape=[jax.ShapeDtypeStruct(a.shape, a.dtype) for a in (rest, own)],
        input_output_aliases={2: 1, 3: 0},
        compiler_params=pltpu.CompilerParams(vmem_limit_bytes=40 * 1024 * 1024),
        name="first_part",
    )(bias, halo, own, rest)[0]


def unpack_kernel(got_ref, out_hbm, out_ref, sems):
    stores = []
    for two in range(FR // 2):
        for head in range(HEADS):
            tiles = [
                got_ref[group * HEADS + head, two * 2 * ROWS : (two + 1) * 2 * ROWS, :].astype(jnp.float32)
                for group in range(got_ref.shape[0] // HEADS)
            ]
            for half in range(2):
                rows = jnp.concatenate([t[half * ROWS : (half + 1) * ROWS] for t in tiles], axis=0)
                out_ref[2 * two + half, :, head * HEAD : (head + 1) * HEAD] = rows.astype(jnp.bfloat16)
        span = slice(2 * two, 2 * two + 2)
        store = pltpu.make_async_copy(out_ref.at[span], out_hbm.at[span], sems.at[two])
        store.start()
        stores.append(store)
    for store in stores:
        store.wait()


def unpack(got):
    shape = (FR, got.shape[0] // HEADS * ROWS, HEADS * HEAD)
    return pl.pallas_call(
        unpack_kernel,
        in_specs=[VMEM],
        out_specs=pl.BlockSpec(memory_space=pl.ANY),
        out_shape=jax.ShapeDtypeStruct(shape, got.dtype),
        scratch_shapes=[pltpu.VMEM(shape, jnp.bfloat16), pltpu.SemaphoreType.DMA((FR // 2,))],
        compiler_params=pltpu.CompilerParams(vmem_limit_bytes=40 * 1024 * 1024),
        name="unpack",
    )(got)


def exchange(array, groups):
    return lax.all_to_all(array, ("inner", "outer"), 0, 0, tiled=True, axis_index_groups=groups)


def on_device(frames, queries, w_keyval, bucket_table, bias_table, block_mask):
    n_outer = lax.axis_size("outer")
    n_blocks = lax.axis_size("inner") * n_outer
    groups = [list(range(g, g + GROUP)) for g in range(0, n_blocks, GROUP)]
    width = frames.shape[3]

    sent = prep(
        frames.reshape(-1, width),
        queries.reshape(-1, queries.shape[3]),
        w_keyval,
        block_mask.reshape(-1),
    )
    got = exchange(sent.reshape(GROUP, MESSAGE, HEAD), groups)
    perm = [(i, i + GROUP) for i in range(n_blocks - GROUP)]
    halo = lax.ppermute(got[GROUP - SPAN :, : 2 * CHUNK, :], ("inner", "outer"), perm)
    rest, bias, own = main_part(bucket_table, bias_table.T, got)
    mixed = first_part(bias, halo, own, rest)
    out = exchange(mixed.reshape(GROUP, CHUNK, HEAD), groups)
    return unpack(out).reshape(queries.shape)


def solution(mesh):
    in_specs = (
        P("outer", "inner", None, None),
        P("outer", "inner", None, None),
        P(),
        P(),
        P(),
        P("outer", "inner", None),
    )
    out_specs = P("outer", "inner", None, None)
    return jax.shard_map(
        on_device, mesh=mesh, in_specs=in_specs, out_specs=out_specs, check_vma=False
    )
```
